32 devices in a mesh: dp: 16 (over z, y, core), band: 2 (over x).
Axes of the slice: x: 2, y: 2, z: 4, core: 2. Of those that a mesh axis runs over, the one named last changes fastest.
Arguments:
- radiance: bfloat16 [16, 280, 32, 128], P('dp', 'band'), may hold values from -6 to 6
- kernel: bfloat16 [280, 7, 7], P('band'), may hold values from -0.875 to 0.875
- w_first: bfloat16 [280, 64], replicated, may hold values from -0.375 to 0.375
- w_mid: bfloat16 [64, 64], replicated, may hold values from -0.75 to 0.75
- w_out: bfloat16 [64, 280], replicated, may hold values from -0.75 to 0.75
- target: bfloat16 [16, 280, 32, 128], P('dp', None, 'band'), may hold values from -6 to 6
- mask: int32 [16, 32, 128], P('dp', 'band'), may hold values 0 or 1
Outputs:
- grad_kernel: float32 [280, 7, 7], P('band')
- grad_first: float32 [280, 64], replicated
- grad_mid: float32 [64, 64], replicated
- grad_out: float32 [64, 280], replicated
The draws below stay inside these ranges and needn't reach their ends.
All inputs are finite; a program needn't handle non-finite values. No bound on the sum of `mask` on one device may be relied on, other than what follows from the above.
Results may differ from the reference program's by a relative error of at most 0.00056.
Values may be sent and summed in bfloat16 or wider, within the bound.
A program may use at most 64 MiB of HBM per device.

```python
import math
import jax
import jax.numpy as jnp
from jax import lax

BANDS = 280
CH = 64
KS = 7
H = 32
W = 128
CROPS = 16


def plant(result, key, smallest, largest):
    place = [jax.random.randint(jax.random.fold_in(key, axis), (), 0, length) for axis, length in enumerate(result.shape)]
    main_axis = result.shape.index(max(result.shape))
    next_to = place[:main_axis] + [(place[main_axis] + 1) % result.shape[main_axis]] + place[main_axis + 1:]
    return result.at[tuple(place)].set(smallest).at[tuple(next_to)].set(largest)


def shard_levels(key, shape, split, low, largest):
    def one(dim, blocks):
        draws = jax.random.uniform(jax.random.fold_in(jax.random.fold_in(key, 6), dim), (blocks,), jnp.float32, low / len(split), largest / len(split))
        return jnp.repeat(jnp.exp(draws), shape[dim] // blocks).reshape((-1,) + (1,) * (len(shape) - dim - 1))

    loudness = one(*split[0])
    for cut in split[1:]:
        loudness = loudness * one(*cut)
    return loudness


def bell_draw(own_key, dims, width, limit, pieces=(), kind=jnp.bfloat16):
    gain = shard_levels(own_key, dims, pieces, -0.22, 0.18) if pieces else 1.0
    result = jax.random.normal(own_key, dims, jnp.float32) * width * gain
    return jnp.minimum(jnp.maximum(result, -limit), limit).astype(kind)


def setup_inputs(seed: int = 0) -> dict:
    key_list = jax.random.split(jax.random.key(seed), 8)
    radiance = bell_draw(key_list[0], (CROPS, BANDS, H, W), 1.0, 6.0, ((0, 16), (1, 2)))
    kernel = bell_draw(key_list[1], (BANDS, KS, KS), (KS * KS) ** -0.5, 0.875, ((0, 2),))
    w_first = bell_draw(key_list[2], (BANDS, CH), BANDS ** -0.5, 0.375)
    w_mid = bell_draw(key_list[3], (CH, CH), CH ** -0.5, 0.75)
    w_out = bell_draw(key_list[4], (CH, BANDS), CH ** -0.5, 0.75)
    target = bell_draw(key_list[5], (CROPS, BANDS, H, W), 1.0, 6.0, ((0, 16), (2, 2)))
    mask = plant((jax.random.randint(key_list[6], (CROPS, H, W), 0, 4) < 3).astype(jnp.int32), jax.random.fold_in(key_list[6], 1), 0, 1)
    return {"radiance": radiance, "kernel": kernel, "w_first": w_first, "w_mid": w_mid, "w_out": w_out, "target": target, "mask": mask}


def spatial(image, kernel):
    out = lax.conv_general_dilated(image[None], kernel[:, None], (1, 1), ((3, 3), (3, 3)), dimension_numbers=('NCHW', 'OIHW', 'NCHW'), feature_group_count=image.shape[0], preferred_element_type=jnp.float32)
    return out[0]

def kernel_slope(image, slope):
    out = lax.conv_general_dilated(image[None], slope[:, None], (1, 1), ((3, 3), (3, 3)), dimension_numbers=('NCHW', 'OIHW', 'NCHW'), feature_group_count=image.shape[0], preferred_element_type=jnp.float32)
    return out[0]

def silu_slope(value):
    sig = jax.nn.sigmoid(value)
    return sig * (1.0 + value * (1.0 - sig))

def reference(radiance, kernel, w_first, w_mid, w_out, target, mask):
    scale = 1.0 / math.sqrt(CROPS * H * W)
    first = w_first.astype(jnp.float32)
    middle = w_mid.astype(jnp.float32)
    outer = w_out.astype(jnp.float32)

    def one_crop(items):
        image, wanted, valid = items
        filtered = spatial(image, kernel).astype(jnp.bfloat16)
        z_first = jnp.einsum('bhw,bc->chw', filtered.astype(jnp.float32), first)
        hid_first = jax.nn.silu(z_first).astype(jnp.bfloat16)
        z_mid = jnp.einsum('chw,cd->dhw', hid_first.astype(jnp.float32), middle)
        hid_mid = (hid_first.astype(jnp.float32) + jax.nn.silu(z_mid)).astype(jnp.bfloat16)
        predicted = jnp.einsum('chw,co->ohw', hid_mid.astype(jnp.float32), outer)
        err = (2.0 * scale * valid.astype(jnp.float32)[None] * (predicted - wanted.astype(jnp.float32))).astype(jnp.bfloat16)
        errf = err.astype(jnp.float32)
        grad_out = jnp.einsum('chw,ohw->co', hid_mid.astype(jnp.float32), errf)
        d_mid = jnp.einsum('co,ohw->chw', outer, errf)
        dz_mid = (d_mid * silu_slope(z_mid)).astype(jnp.bfloat16)
        grad_mid = jnp.einsum('chw,dhw->cd', hid_first.astype(jnp.float32), dz_mid.astype(jnp.float32))
        d_first = d_mid + jnp.einsum('cd,dhw->chw', middle, dz_mid.astype(jnp.float32))
        dz_first = (d_first * silu_slope(z_first)).astype(jnp.bfloat16)
        grad_first = jnp.einsum('bhw,chw->bc', filtered.astype(jnp.float32), dz_first.astype(jnp.float32))
        slope = jnp.einsum('bc,chw->bhw', first, dz_first.astype(jnp.float32)).astype(jnp.bfloat16)
        grad_kernel = kernel_slope(image, slope)
        return (grad_kernel, grad_first, grad_mid, grad_out)
    parts = lax.map(one_crop, (radiance, target, mask))
    return (lax.optimization_barrier(jnp.sum(parts[0], axis=0)), lax.optimization_barrier(jnp.sum(parts[1], axis=0)), lax.optimization_barrier(jnp.sum(parts[2], axis=0)), lax.optimization_barrier(jnp.sum(parts[3], axis=0)))
```

```python
import functools
import math

import jax
import jax.numpy as jnp
from jax import lax
from jax.experimental import pallas as pl
from jax.experimental.pallas import tpu as pltpu
from jax.sharding import PartitionSpec as P

MESH = pl.DeviceIdType.MESH
F32 = jnp.float32
BF16 = jnp.bfloat16
PACK = 4


def up(value, step):
    return -(-value // step) * step


def mm(a, b):
    return jnp.dot(a, b, preferred_element_type=F32)


def mm_nt(a, b):
    return lax.dot_general(a, b, (((1,), (1,)), ((), ())), preferred_element_type=F32)


def kernel(
    cfg,
    x_ref, taps_ref, wft_ref, wf_ref, wm_ref, wmt_ref, wo_ref, wot_ref, target_ref, mask_ref,
    gk_ref, gf_ref, gm_ref, go_ref,
    stack, filt, slope, z_send, z_recv, dz_all, hid_s,
    early, early_in, early_out, late, late_in,
    z_ss, z_rs, d_ss, d_rs, e_ss, e_rs, ea_ss, ea_rs, l_ss, l_rs, la_ss, la_rs,
):
    nd, nb = cfg["nd"], cfg["nb"]
    bands, groups, bp, ks = cfg["bands"], cfg["groups"], cfg["bp"], cfg["ks"]
    rows_all, rows, width, chunks = cfg["rows_all"], cfg["rows"], cfg["width"], cfg["chunks"]
    ch, outs, scale = cfg["ch"], cfg["outs"], cfg["scale"]
    ew, lw = cfg["ew"], cfg["lw"]
    half = ks // 2
    lanes = 8 * rows_all
    step_rows = rows // chunks
    me_d = lax.axis_index("dp")
    me_b = lax.axis_index("band")
    me = me_d * nb + me_b
    total = nd * nb

    def device(index):
        return (index // nb, lax.rem(index, nb))

    barrier = pltpu.get_barrier_semaphore()

    def greet(k, _):
        pl.semaphore_signal(
            barrier, inc=1, device_id=device(lax.rem(me + k, total)), device_id_type=MESH
        )
        return 0

    lax.fori_loop(1, total, greet, 0)

    row_i = lax.broadcasted_iota(jnp.int32, (rows_all, lanes), 0)
    lane_i = lax.broadcasted_iota(jnp.int32, (rows_all, lanes), 1)
    block = lane_i // rows_all
    tap = lane_i % rows_all - row_i + half
    band_mask = (tap >= 0) & (tap < ks) & (block < ks)
    col = lax.broadcasted_iota(jnp.int32, (rows_all, width), 1)
    tail = bp - 16
    for h in range(rows_all):
        filt[pl.ds(h * bp + tail, 16), :] = jnp.zeros((16, width), F32)

    def filter_group(g, _):
        packed = pltpu.roll(taps_ref[pl.ds(g, 1), :], 8 - half, 1)
        spread = jnp.broadcast_to(packed, (rows_all, lanes))
        for q in range(PACK):
            b = jnp.minimum(g * PACK + q, bands - 1)
            image = x_ref[b].astype(F32)
            parts = []
            for j in range(ks):
                s = j - half
                if s == 0:
                    moved = image
                else:
                    moved = pltpu.roll(image, (-s) % width, 1)
                    moved = jnp.where((col + s >= 0) & (col + s < width), moved, 0.0)
                parts.append(moved.astype(BF16))
            parts.append(jnp.zeros((lanes - ks * rows_all, width), BF16))
            moved_all = jnp.concatenate(parts, axis=0)
            stack[g * PACK + q] = moved_all
            taps = pltpu.roll(
                spread, lanes - 8 - 8 * q, 1, stride=1, stride_axis=0
            )
            taps = jnp.where(band_mask, taps, 0.0).astype(BF16)
            out = mm(taps, moved_all)
            filt[pl.ds(g * PACK + q, rows_all, stride=bp), :] = out.astype(BF16).astype(F32)
        return 0

    lax.fori_loop(0, groups, filter_group, 0)

    def filt_rows(h, count):
        return jnp.concatenate(
            [
                filt[pl.ds(pl.multiple_of((h + r) * bp, 8), bp), :].astype(BF16)
                for r in range(count)
            ],
            axis=1,
        )

    pl.semaphore_wait(barrier, total - 1)

    def z_copy(k, c):
        part = pl.ds(c * step_rows, step_rows)
        return pltpu.make_async_remote_copy(
            src_ref=z_send.at[k, part],
            dst_ref=z_recv.at[k, part],
            send_sem=z_ss.at[k, c],
            recv_sem=z_rs.at[k, c],
            device_id=(me_d, lax.rem(me_b + k, nb)),
            device_id_type=MESH,
        )

    def z_part(k, c):
        owner = lax.rem(me_b + k, nb)

        def one(p, _):
            h = c * step_rows + p * 2
            z = mm(wft_ref[...], filt_rows(owner * rows + h, 2))
            z_send[k, h] = z[:, :width]
            z_send[k, h + 1] = z[:, width:]
            return 0

        lax.fori_loop(0, step_rows // 2, one, 0, unroll=True)

    for k in range(1, nb):
        for c in range(chunks):
            z_part(k, c)
            z_copy(k, c).start()
    for c in range(chunks):
        z_part(0, c)

    def d_copy(k, c):
        part = pl.ds(me_b * rows + c * step_rows, step_rows)
        return pltpu.make_async_remote_copy(
            src_ref=dz_all.at[part],
            dst_ref=dz_all.at[part],
            send_sem=d_ss.at[k, c],
            recv_sem=d_rs.at[k, c],
            device_id=(me_d, lax.rem(me_b + k, nb)),
            device_id_type=MESH,
        )

    def wide(pieces):
        return jnp.concatenate(pieces, axis=1)

    g_out = jnp.zeros((ch, outs), F32)
    g_mid = jnp.zeros((ch, ch), F32)
    for c in range(chunks):
        for k in range(1, nb):
            z_copy(k, c).wait_recv()
        z_list = []
        for r in range(step_rows):
            h = c * step_rows + r
            z = z_send[0, h]
            for k in range(1, nb):
                z = z + z_recv[k, h]
            z_list.append(z)
        z_first = wide(z_list)
        sig_first = jax.nn.sigmoid(z_first)
        hid_first = (z_first * sig_first).astype(BF16)
        z_mid = mm(wmt_ref[...], hid_first)
        sig_mid = jax.nn.sigmoid(z_mid)
        hid_mid = (hid_first.astype(F32) + z_mid * sig_mid).astype(BF16)
        predicted = mm(wot_ref[...], hid_mid)
        errs = []
        for r in range(step_rows):
            h = c * step_rows + r
            factor = (2.0 * scale) * mask_ref[pl.ds(h, 1), :].astype(F32)
            diff = predicted[:, r * width:(r + 1) * width] - target_ref[h].astype(F32)
            errs.append((factor * diff).astype(BF16))
        err = wide(errs)
        g_out = g_out + mm_nt(hid_mid, err)
        d_mid = mm(wo_ref[...], err)
        dz_mid = (d_mid * (sig_mid * (1.0 + z_mid * (1.0 - sig_mid)))).astype(BF16)
        g_mid = g_mid + mm_nt(hid_first, dz_mid)
        d_first = d_mid + mm(wm_ref[...], dz_mid)
        dz = (d_first * (sig_first * (1.0 + z_first * (1.0 - sig_first)))).astype(BF16)
        for r in range(step_rows):
            h = c * step_rows + r
            dz_all[me_b * rows + h] = dz[:, r * width:(r + 1) * width]
        for k in range(1, nb):
            d_copy(k, c).start()

    hid_s[...] = jnp.zeros_like(hid_s)

    def slope_rows(first):
        def one(p, _):
            h = first + 2 * p
            dz = wide([dz_all[h], dz_all[h + 1]])
            hid_s[...] += mm_nt(dz, filt_rows(h, 2))
            back = mm(wf_ref[...], dz)
            for r in range(2):
                place = pl.multiple_of((rows_all - 1 - h - r) * bp, 8)
                slope[pl.ds(place, bp), :] = back[:, r * width:(r + 1) * width]
            return 0

        lax.fori_loop(0, step_rows // 2, one, 0, unroll=True)

    for c in range(chunks):
        slope_rows(me_b * rows + c * step_rows)
    for k in range(1, nb):
        source = lax.rem(me_b + nb - k, nb)
        for c in range(chunks):
            d_copy(k, c).wait_recv()
            slope_rows(source * rows + c * step_rows)

    def piece(ref, index, w):
        lane_parts = nd // 8
        each = w // lane_parts
        return ref.at[
            pl.ds(pl.multiple_of((index // lane_parts) * 8, 8), 8),
            pl.ds(pl.multiple_of(lax.rem(index, lane_parts) * each, 128), each),
        ]

    def scatter_copy(ref, into, w, ss, rs, k):
        peer = lax.rem(me_d + k, nd)
        return pltpu.make_async_remote_copy(
            src_ref=piece(ref, peer, w),
            dst_ref=into.at[k],
            send_sem=ss.at[k],
            recv_sem=rs.at[k],
            device_id=(peer, me_b),
            device_id_type=MESH,
        )

    def each(count, act):
        def body(k, _):
            act(k)
            return 0

        lax.fori_loop(1, count, body, 0)

    def gather_early(k):
        part = piece(early_out.at[me_b], me_d, ew)
        return pltpu.make_async_remote_copy(
            src_ref=part,
            dst_ref=part,
            send_sem=ea_ss.at[k],
            recv_sem=ea_rs.at[k],
            device_id=device(lax.rem(me + k, total)),
            device_id_type=MESH,
        )

    def gather_late(k):
        part = piece(gk_ref, me_d, lw)
        return pltpu.make_async_remote_copy(
            src_ref=part,
            dst_ref=part,
            send_sem=la_ss.at[k],
            recv_sem=la_rs.at[k],
            device_id=(lax.rem(me_d + k, nd), me_b),
            device_id_type=MESH,
        )

    early[...] = jnp.zeros_like(early)
    early[:, 0:outs] = g_out
    early[:, outs:outs + ch] = g_mid
    early[:, outs + ch:outs + ch + bands] = hid_s[:, 0:bands]
    each(nd, lambda k: scatter_copy(early, early_in, ew, e_ss, e_rs, k).start())
    late[...] = jnp.zeros_like(late)

    h_i = rows_all - 1 - row_i
    skew = lanes - (rows_all - 1) + half
    extra = -skew % 8
    lane_e = jnp.maximum(lane_i - extra, 0)
    block_e = jnp.where(lane_i >= extra, lane_e // rows_all, ks)
    tap_e = lane_e % rows_all

    def taps_group(g, _):
        acc = jnp.zeros((rows_all, lanes), F32)
        for q in range(PACK):
            b = g * PACK + q
            rows_b = slope[pl.ds(b, rows_all, stride=bp), :].astype(BF16)
            cross = mm_nt(rows_b, stack[b])
            place = 8 * q
            moved = pltpu.roll(
                cross, (skew + extra + place) % lanes, 1, stride=1, stride_axis=0
            )
            i = tap_e - place
            source = h_i + i - half
            valid = (i >= 0) & (i < ks) & (source >= 0) & (source < rows_all) & (block_e < ks)
            acc = acc + jnp.where(valid, moved, 0.0)
        summed = jnp.sum(acc, axis=0, keepdims=True)
        late[pl.ds(g, 1), 0:lanes] = pltpu.roll(summed, lanes - extra, 1)
        return 0

    cut = groups // 2
    lax.fori_loop(0, cut, taps_group, 0)

    each(nd, lambda k: scatter_copy(early, early_in, ew, e_ss, e_rs, k).wait_recv())
    own = piece(early, me_d, ew)[...]
    for k in range(1, nd):
        own = own + early_in[k]
    piece(early_out.at[me_b], me_d, ew)[...] = own
    each(total, lambda k: gather_early(k).start())

    lax.fori_loop(cut, groups, taps_group, 0)

    each(nd, lambda k: scatter_copy(late, late_in, lw, l_ss, l_rs, k).start())
    each(total, lambda k: gather_early(k).wait_recv())
    result = early_out[0]
    for k in range(1, nb):
        result = result + early_out[k]
    go_ref[...] = result[:, 0:outs]
    gm_ref[...] = result[:, outs:outs + ch]
    for k in range(nb):
        gf_ref[:, k * bands:(k + 1) * bands] = early_out[k, :, outs + ch:outs + ch + bands]

    each(nd, lambda k: scatter_copy(late, late_in, lw, l_ss, l_rs, k).wait_recv())
    own = piece(late, me_d, lw)[...]
    for k in range(1, nd):
        own = own + late_in[k]
    piece(gk_ref, me_d, lw)[...] = own
    each(nd, lambda k: gather_late(k).start())
    each(nd, lambda k: gather_late(k).wait_recv())

    for k in range(1, nb):
        for c in range(chunks):
            z_copy(k, c).wait_send()
            d_copy(k, c).wait_send()
    each(nd, lambda k: scatter_copy(early, early_in, ew, e_ss, e_rs, k).wait_send())
    each(total, lambda k: gather_early(k).wait_send())
    each(nd, lambda k: scatter_copy(late, late_in, lw, l_ss, l_rs, k).wait_send())
    each(nd, lambda k: gather_late(k).wait_send())


def on_device(nd, nb, radiance, kernel_taps, w_first, w_mid, w_out, target, mask):
    image = radiance[0]
    bands, rows_all, width = image.shape
    ks = kernel_taps.shape[1]
    ch = w_first.shape[1]
    outs = w_out.shape[1]
    rows = rows_all // nb
    chunks = 2
    groups = -(-bands // PACK)
    bp = up(groups * PACK, 16)
    lane_parts = nd // 8
    ew = up(outs + ch + bands, 128 * lane_parts)
    lw = up(8 * rows_all, 128 * lane_parts)
    cfg = dict(
        nd=nd, nb=nb, bands=bands, groups=groups, bp=bp, ks=ks, rows_all=rows_all, rows=rows,
        width=width, chunks=chunks, ch=ch, outs=outs, ew=ew, lw=lw,
        scale=1.0 / math.sqrt(nd * rows_all * width),
    )
    taps = jnp.pad(kernel_taps, ((0, groups * PACK - bands), (0, 8 - ks), (0, 8 - ks)))
    taps = taps.reshape(groups, PACK, 8, 8).transpose(0, 3, 1, 2).reshape(groups, 8 * PACK * 8)
    own = lax.dynamic_slice_in_dim(w_first, lax.axis_index("band") * bands, bands, 0)
    own = jnp.pad(own, ((0, bp - bands), (0, 0)))
    sems = lambda *shape: pltpu.SemaphoreType.DMA(shape)
    lanes = 8 * rows_all
    packed, g_first, g_mid, g_out = pl.pallas_call(
        functools.partial(kernel, cfg),
        out_shape=(
            jax.ShapeDtypeStruct((64, lw), F32),
            jax.ShapeDtypeStruct((ch, bands * nb), F32),
            jax.ShapeDtypeStruct((ch, ch), F32),
            jax.ShapeDtypeStruct((ch, outs), F32),
        ),
        in_specs=[pl.BlockSpec(memory_space=pltpu.VMEM)] * 10,
        out_specs=(pl.BlockSpec(memory_space=pltpu.VMEM),) * 4,
        scratch_shapes=[
            pltpu.VMEM((groups * PACK, lanes, width), BF16),
            pltpu.VMEM((rows_all * bp, width), F32),
            pltpu.VMEM((rows_all * bp, width), F32),
            pltpu.VMEM((nb, rows, ch, width), F32),
            pltpu.VMEM((nb, rows, ch, width), F32),
            pltpu.VMEM((rows_all, ch, width), BF16),
            pltpu.VMEM((ch, bp), F32),
            pltpu.VMEM((64, ew), F32),
            pltpu.VMEM((nd, 8, ew // lane_parts), F32),
            pltpu.VMEM((nb, 64, ew), F32),
            pltpu.VMEM((64, lw), F32),
            pltpu.VMEM((nd, 8, lw // lane_parts), F32),
            sems(nb, chunks), sems(nb, chunks), sems(nb, chunks), sems(nb, chunks),
            sems(nd), sems(nd), sems(nd * nb), sems(nd * nb),
            sems(nd), sems(nd), sems(nd), sems(nd),
        ],
        compiler_params=pltpu.CompilerParams(
            collective_id=0, has_side_effects=True, vmem_limit_bytes=56 * 1024 * 1024
        ),
    )(
        image, taps.astype(F32), own.T, own, w_mid, w_mid.T, w_out, w_out.T,
        target[0].transpose(1, 0, 2), mask[0],
    )
    g_taps = packed[:groups, :lanes].reshape(groups, 8, PACK, 8).transpose(0, 2, 3, 1)
    g_taps = g_taps.reshape(groups * PACK, 8, 8)[:bands, :ks, :ks]
    return (g_taps, g_first.T, g_mid, g_out)


def solution(mesh):
    in_specs = (
        P("dp", "band", None, None),
        P("band", None, None),
        P(),
        P(),
        P(),
        P("dp", None, "band", None),
        P("dp", "band", None),
    )
    out_specs = (P("band", None, None), P(), P(), P())
    return jax.shard_map(
        functools.partial(on_device, mesh.shape["dp"], mesh.shape["band"]),
        mesh=mesh, in_specs=in_specs, out_specs=out_specs, check_vma=False,
    )
```

```python
import functools
import math

import jax
import jax.numpy as jnp
from jax import lax
from jax.experimental import pallas as pl
from jax.experimental.pallas import tpu as pltpu
from jax.sharding import PartitionSpec as P

MESH = pl.DeviceIdType.MESH
F32 = jnp.float32
BF16 = jnp.bfloat16


def up(value, step):
    return -(-value // step) * step


def mm(a, b):
    return jnp.dot(a, b, preferred_element_type=F32)


def mm_tn(a, b):
    return lax.dot_general(a, b, (((0,), (0,)), ((), ())), preferred_element_type=F32)


def eye(n):
    same = lax.broadcasted_iota(jnp.int32, (n, n), 0) == lax.broadcasted_iota(jnp.int32, (n, n), 1)
    return jnp.where(same, 1.0, 0.0).astype(BF16)


def mm_nt(a, b):
    return lax.dot_general(a, b, (((1,), (1,)), ((), ())), preferred_element_type=F32)


def kernel(
    cfg,
    x_ref, taps_ref, w1t_ref, wm_ref, wo_ref, target_ref, mask_ref,
    gk_ref, gf_ref, gm_ref, go_ref,
    tap_rows, taps_own, wft_ref, wf_ref, wmt_ref, wot_ref, wanted, sums, stack, filt, slope, z_send, z_recv, dz_all, hid_s,
    early, early_in, early_out, late, late_in,
    z_ss, z_rs, d_ss, d_rs, e_ss, e_rs, ea_ss, ea_rs, l_ss, l_rs, la_ss, la_rs,
):
    nd, nb = cfg["nd"], cfg["nb"]
    bands, unroll, bp, ks = cfg["bands"], cfg["unroll"], cfg["bp"], cfg["ks"]
    rows_all, rows, width, chunks = cfg["rows_all"], cfg["rows"], cfg["width"], cfg["chunks"]
    ch, outs, scale = cfg["ch"], cfg["outs"], cfg["scale"]
    ew, lw = cfg["ew"], cfg["lw"]
    half = ks // 2
    lanes = 8 * rows_all
    step_rows = rows // chunks
    me_d = lax.axis_index("dp")
    me_b = lax.axis_index("band")
    me = me_d * nb + me_b
    total = nd * nb
    split = nb == 2

    def device(index):
        return (index // nb, lax.rem(index, nb))

    barrier = pltpu.get_barrier_semaphore()

    def greet(k, _):
        pl.semaphore_signal(
            barrier, inc=1, device_id=device(lax.rem(me + k, total)), device_id_type=MESH
        )
        return 0

    lax.fori_loop(1, total, greet, 0)

    row_i = lax.broadcasted_iota(jnp.int32, (rows_all, lanes), 0)
    lane_i = lax.broadcasted_iota(jnp.int32, (rows_all, lanes), 1)
    block = lane_i // rows_all
    tap = lane_i % rows_all - row_i + half
    band_mask = (tap >= 0) & (tap < ks) & (block < ks)
    col = lax.broadcasted_iota(jnp.int32, (rows_all, width), 1)
    for h in range(rows_all):
        filt[pl.ds(h * bp + bp - 16, 16), :] = jnp.zeros((16, width), F32)

    place_j = lax.broadcasted_iota(jnp.int32, (ks, lanes), 0)
    place_l = lax.broadcasted_iota(jnp.int32, (ks, lanes), 1) - (8 - half)
    base = jnp.zeros((bands, lanes), F32)
    for i in range(ks):
        spot = jnp.where(place_l == place_j * rows_all + i, 1.0, 0.0).astype(BF16)
        base = base + mm_tn(taps_ref[i], spot)
    tap_rows[0:bands, :] = base

    lower = me_b == 0
    mid_row = rows_all // 2

    def filter_band(b):
        image = x_ref[b]
        parts = []
        for j in range(ks):
            s = j - half
            if s == 0:
                moved = image
            else:
                moved = pltpu.roll(image, (-s) % width, 1)
                moved = jnp.where((col + s >= 0) & (col + s < width), moved, jnp.zeros((), BF16))
            parts.append(moved)
        parts.append(jnp.zeros((lanes - ks * rows_all, width), BF16))
        moved_all = jnp.concatenate(parts, axis=0)
        stack[b] = moved_all
        spread = jnp.broadcast_to(tap_rows[pl.ds(b, 1), :], (rows_all, lanes))
        taps = pltpu.roll(spread, lanes - 8, 1, stride=1, stride_axis=0)
        taps = jnp.where(band_mask, taps, 0.0)
        if split:
            taps_own[b] = jnp.where(lower, taps[:mid_row], taps[mid_row:]).astype(BF16)
            taps = jnp.where(lower, taps[mid_row:], taps[:mid_row])
            first, count = (1 - me_b) * rows, rows
        else:
            first, count = 0, rows_all
        out = mm(taps.astype(BF16), moved_all)
        filt[pl.ds(first * bp + b, count, stride=bp), :] = out.astype(BF16).astype(F32)

    def filter_own(b):
        out = mm(taps_own[b], stack[b])
        filt[pl.ds(me_b * rows * bp + b, rows, stride=bp), :] = out.astype(BF16).astype(F32)

    def over_bands(lo, hi, act):
        def body(g, _):
            for q in range(unroll):
                act(g * unroll + q)
            return 0

        lax.fori_loop(lo, hi, body, 0)

    groups = bands // unroll
    over_bands(0, groups, filter_band)

    pick = jnp.where(
        lax.broadcasted_iota(jnp.int32, (bp, outs), 1)
        == lax.broadcasted_iota(jnp.int32, (bp, outs), 0) + me_b * bands,
        1.0, 0.0,
    )
    pick = jnp.where(lax.broadcasted_iota(jnp.int32, (bp, outs), 0) < bands, pick, 0.0).astype(BF16)
    wft_ref[...] = mm_nt(w1t_ref[...], pick).astype(BF16)

    def filt_rows(h, count):
        return jnp.concatenate(
            [
                filt[pl.ds(pl.multiple_of((h + r) * bp, 8), bp), :].astype(BF16)
                for r in range(count)
            ],
            axis=1,
        )

    pl.semaphore_wait(barrier, total - 1)

    def z_copy(k, c):
        part = pl.ds(c * step_rows, step_rows)
        return pltpu.make_async_remote_copy(
            src_ref=z_send.at[k, part],
            dst_ref=z_recv.at[k, part],
            send_sem=z_ss.at[k, c],
            recv_sem=z_rs.at[k, c],
            device_id=(me_d, lax.rem(me_b + k, nb)),
            device_id_type=MESH,
        )

    def z_part(k, c):
        owner = lax.rem(me_b + k, nb)

        def one(p, _):
            h = c * step_rows + p * 2
            z = mm(wft_ref[...], filt_rows(owner * rows + h, 2))
            z_send[k, h] = z[:, :width]
            z_send[k, h + 1] = z[:, width:]
            return 0

        lax.fori_loop(0, step_rows // 2, one, 0, unroll=True)

    for k in range(1, nb):
        for c in range(chunks):
            z_part(k, c)
            z_copy(k, c).start()
    if split:
        over_bands(0, groups, filter_own)
    for c in range(chunks):
        z_part(0, c)
    wf_ref[...] = mm_nt(pick, w1t_ref[...]).astype(BF16)
    wmt_ref[...] = mm_nt(eye(ch), wm_ref[...]).astype(BF16)
    wot_ref[...] = mm_nt(eye(outs), wo_ref[...]).astype(BF16)
    wanted[...] = target_ref[...].astype(F32)

    def d_copy(k, c):
        part = pl.ds(me_b * rows + c * step_rows, step_rows)
        return pltpu.make_async_remote_copy(
            src_ref=dz_all.at[part],
            dst_ref=dz_all.at[part],
            send_sem=d_ss.at[k, c],
            recv_sem=d_rs.at[k, c],
            device_id=(me_d, lax.rem(me_b + k, nb)),
            device_id_type=MESH,
        )

    def wide(pieces):
        return jnp.concatenate(pieces, axis=1)

    g_out = jnp.zeros((ch, outs), F32)
    g_mid = jnp.zeros((ch, ch), F32)
    for c in range(chunks):
        for k in range(1, nb):
            z_copy(k, c).wait_recv()
        z_list = []
        for r in range(step_rows):
            h = c * step_rows + r
            z = z_send[0, h]
            for k in range(1, nb):
                z = z + z_recv[k, h]
            z_list.append(z)
        z_first = wide(z_list)
        sig_first = jax.nn.sigmoid(z_first)
        hid_first = (z_first * sig_first).astype(BF16)
        z_mid = mm(wmt_ref[...], hid_first)
        sig_mid = jax.nn.sigmoid(z_mid)
        hid_mid = (hid_first.astype(F32) + z_mid * sig_mid).astype(BF16)
        predicted = mm(wot_ref[...], hid_mid)
        errs = []
        for r in range(step_rows):
            h = c * step_rows + r
            factor = (2.0 * scale) * mask_ref[pl.ds(h, 1), :].astype(F32)
            diff = predicted[:, r * width:(r + 1) * width] - wanted[pl.ds(h, outs, stride=rows), :]
            errs.append((factor * diff).astype(BF16))
        err = wide(errs)
        g_out = g_out + mm_nt(hid_mid, err)
        d_mid = mm(wo_ref[...], err)
        dz_mid = (d_mid * (sig_mid * (1.0 + z_mid * (1.0 - sig_mid)))).astype(BF16)
        g_mid = g_mid + mm_nt(hid_first, dz_mid)
        d_first = d_mid + mm(wm_ref[...], dz_mid)
        dz = (d_first * (sig_first * (1.0 + z_first * (1.0 - sig_first)))).astype(BF16)
        for r in range(step_rows):
            h = c * step_rows + r
            dz_all[me_b * rows + h] = dz[:, r * width:(r + 1) * width]
        for k in range(1, nb):
            d_copy(k, c).start()

    hid_s[...] = jnp.zeros_like(hid_s)

    def slope_rows(first):
        def one(p, _):
            h = first + 2 * p
            dz = wide([dz_all[h], dz_all[h + 1]])
            hid_s[...] += mm_nt(dz, filt_rows(h, 2))
            back = mm(wf_ref[...], dz)
            for r in range(2):
                place = pl.multiple_of((rows_all - 1 - h - r) * bp, 8)
                slope[pl.ds(place, bp), :] = back[:, r * width:(r + 1) * width]
            return 0

        lax.fori_loop(0, step_rows // 2, one, 0, unroll=True)

    for c in range(chunks):
        slope_rows(me_b * rows + c * step_rows)
    for k in range(1, nb):
        source = lax.rem(me_b + nb - k, nb)
        for c in range(chunks):
            d_copy(k, c).wait_recv()
            slope_rows(source * rows + c * step_rows)

    def piece(ref, index, w):
        lane_parts = nd // 8
        each = w // lane_parts
        return ref.at[
            pl.ds(pl.multiple_of((index // lane_parts) * 8, 8), 8),
            pl.ds(pl.multiple_of(lax.rem(index, lane_parts) * each, 128), each),
        ]

    def scatter_copy(ref, into, w, ss, rs, k):
        peer = lax.rem(me_d + k, nd)
        return pltpu.make_async_remote_copy(
            src_ref=piece(ref, peer, w),
            dst_ref=into.at[k],
            send_sem=ss.at[k],
            recv_sem=rs.at[k],
            device_id=(peer, me_b),
            device_id_type=MESH,
        )

    def each(count, act):
        def body(k, _):
            act(k)
            return 0

        lax.fori_loop(1, count, body, 0)

    def gather_early(k):
        part = piece(early_out.at[me_b], me_d, ew)
        return pltpu.make_async_remote_copy(
            src_ref=part,
            dst_ref=part,
            send_sem=ea_ss.at[k],
            recv_sem=ea_rs.at[k],
            device_id=device(lax.rem(me + k, total)),
            device_id_type=MESH,
        )

    def gather_late(k):
        part = piece(gk_ref, me_d, lw)
        return pltpu.make_async_remote_copy(
            src_ref=part,
            dst_ref=part,
            send_sem=la_ss.at[k],
            recv_sem=la_rs.at[k],
            device_id=(lax.rem(me_d + k, nd), me_b),
            device_id_type=MESH,
        )

    early[...] = jnp.zeros_like(early)
    early[:, 0:outs] = g_out
    early[:, outs:outs + ch] = g_mid
    early[:, outs + ch:outs + ch + bands] = hid_s[:, 0:bands]
    each(nd, lambda k: scatter_copy(early, early_in, ew, e_ss, e_rs, k).start())
    late[...] = jnp.zeros_like(late)

    h_i = rows_all - 1 - row_i
    skew = lanes - (rows_all - 1) + half
    extra = -skew % 8
    lane_e = jnp.maximum(lane_i - extra, 0)
    tap_e = lane_e % rows_all
    source_e = h_i + tap_e - half
    valid = (
        (lane_i >= extra) & (lane_e // rows_all < ks) & (tap_e < ks)
        & (source_e >= 0) & (source_e < rows_all)
    )
    sums[...] = jnp.zeros_like(sums)

    def taps_band(b):
        rows_b = slope[pl.ds(b, rows_all, stride=bp), :].astype(BF16)
        cross = mm_nt(rows_b, stack[b])
        moved = pltpu.roll(cross, (skew + extra) % lanes, 1, stride=1, stride_axis=0)
        sums[pl.ds(b, 1), :] = jnp.sum(jnp.where(valid, moved, 0.0), axis=0, keepdims=True)

    cut = groups // 2
    over_bands(0, cut, taps_band)

    each(nd, lambda k: scatter_copy(early, early_in, ew, e_ss, e_rs, k).wait_recv())
    own = piece(early, me_d, ew)[...]
    for k in range(1, nd):
        own = own + early_in[k]
    piece(early_out.at[me_b], me_d, ew)[...] = own
    each(total, lambda k: gather_early(k).start())

    over_bands(cut, groups, taps_band)

    slot = (8 * ks, lanes)
    slot_r = lax.broadcasted_iota(jnp.int32, slot, 0)
    slot_l = lax.broadcasted_iota(jnp.int32, slot, 1) - extra
    spot = jnp.where(slot_l == (slot_r % 8) * rows_all + slot_r // 8, 1.0, 0.0)
    late[0:8 * ks, 0:bp] = lax.dot_general(
        spot, sums[...], (((1,), (1,)), ((), ())),
        preferred_element_type=F32, precision=lax.Precision.HIGHEST,
    )

    each(nd, lambda k: scatter_copy(late, late_in, lw, l_ss, l_rs, k).start())
    each(total, lambda k: gather_early(k).wait_recv())
    result = early_out[0]
    for k in range(1, nb):
        result = result + early_out[k]
    go_ref[...] = result[:, 0:outs]
    gm_ref[...] = result[:, outs:outs + ch]
    for k in range(nb):
        gf_ref[:, k * bands:(k + 1) * bands] = early_out[k, :, outs + ch:outs + ch + bands]

    each(nd, lambda k: scatter_copy(late, late_in, lw, l_ss, l_rs, k).wait_recv())
    own = piece(late, me_d, lw)[...]
    for k in range(1, nd):
        own = own + late_in[k]
    piece(gk_ref, me_d, lw)[...] = own
    each(nd, lambda k: gather_late(k).start())
    each(nd, lambda k: gather_late(k).wait_recv())

    for k in range(1, nb):
        for c in range(chunks):
            z_copy(k, c).wait_send()
            d_copy(k, c).wait_send()
    each(nd, lambda k: scatter_copy(early, early_in, ew, e_ss, e_rs, k).wait_send())
    each(total, lambda k: gather_early(k).wait_send())
    each(nd, lambda k: scatter_copy(late, late_in, lw, l_ss, l_rs, k).wait_send())
    each(nd, lambda k: gather_late(k).wait_send())


def finish(gk_in, gf_in, gm_in, go_in, gk_out, gf_out, gm_out, go_out):
    ks, _, bands = gk_out.shape
    for i in range(ks):
        gk_out[i] = gk_in[8 * i:8 * i + ks, 0:bands]
    gf_out[...] = gf_in[...]
    gm_out[...] = gm_in[...]
    go_out[...] = go_in[...]


def on_device(nd, nb, radiance, kernel_taps, w_first, w_mid, w_out, target, mask):
    image = radiance[0]
    bands, rows_all, width = image.shape
    ks = kernel_taps.shape[1]
    ch = w_first.shape[1]
    outs = w_out.shape[1]
    rows = rows_all // nb
    chunks = min(4, rows // 2)
    unroll = max(u for u in range(1, 11) if bands % u == 0)
    bp = up(bands, 16)
    lane_parts = nd // 8
    lanes = 8 * rows_all
    ew = up(outs + ch + bands, 128 * lane_parts)
    lw = up(bp, 128 * lane_parts)
    cfg = dict(
        nd=nd, nb=nb, bands=bands, unroll=unroll, bp=bp, ks=ks, rows_all=rows_all, rows=rows,
        width=width, chunks=chunks, ch=ch, outs=outs, ew=ew, lw=lw,
        scale=1.0 / math.sqrt(nd * rows_all * width),
    )
    sems = lambda *shape: pltpu.SemaphoreType.DMA(shape)
    vmem = pl.BlockSpec(memory_space=pltpu.VMEM)
    sums = pl.pallas_call(
        functools.partial(kernel, cfg),
        out_shape=(
            jax.ShapeDtypeStruct((64, lw), F32),
            jax.ShapeDtypeStruct((ch, bands * nb), F32),
            jax.ShapeDtypeStruct((ch, ch), F32),
            jax.ShapeDtypeStruct((ch, outs), F32),
        ),
        in_specs=[vmem] * 7,
        out_specs=(vmem,) * 4,
        scratch_shapes=[
            pltpu.VMEM((bp, lanes), F32),
            pltpu.VMEM((bands, rows_all // 2, lanes), BF16),
            pltpu.VMEM((ch, bp), BF16),
            pltpu.VMEM((bp, ch), BF16),
            pltpu.VMEM((ch, ch), BF16),
            pltpu.VMEM((outs, ch), BF16),
            pltpu.VMEM((outs * rows, width), F32),
            pltpu.VMEM((bp, lanes), F32),
            pltpu.VMEM((bands, lanes, width), BF16),
            pltpu.VMEM((rows_all * bp, width), F32),
            pltpu.VMEM((rows_all * bp, width), F32),
            pltpu.VMEM((nb, rows, ch, width), F32),
            pltpu.VMEM((nb, rows, ch, width), F32),
            pltpu.VMEM((rows_all, ch, width), BF16),
            pltpu.VMEM((ch, bp), F32),
            pltpu.VMEM((64, ew), F32),
            pltpu.VMEM((nd, 8, ew // lane_parts), F32),
            pltpu.VMEM((nb, 64, ew), F32),
            pltpu.VMEM((64, lw), F32),
            pltpu.VMEM((nd, 8, lw // lane_parts), F32),
            sems(nb, chunks), sems(nb, chunks), sems(nb, chunks), sems(nb, chunks),
            sems(nd), sems(nd), sems(nd * nb), sems(nd * nb),
            sems(nd), sems(nd), sems(nd), sems(nd),
        ],
        compiler_params=pltpu.CompilerParams(
            collective_id=0, has_side_effects=True, vmem_limit_bytes=56 * 1024 * 1024
        ),
    )(
        image, kernel_taps.transpose(1, 2, 0), w_first.T, w_mid, w_out,
        target[0].reshape(outs * rows, width), mask[0],
    )
    g_taps, g_first, g_mid, g_out = pl.pallas_call(
        finish,
        out_shape=(
            jax.ShapeDtypeStruct((ks, ks, bands), F32),
            jax.ShapeDtypeStruct((ch, bands * nb), F32),
            jax.ShapeDtypeStruct((ch, ch), F32),
            jax.ShapeDtypeStruct((ch, outs), F32),
        ),
        in_specs=[vmem] * 4,
        out_specs=(vmem,) * 4,
    )(*sums)
    return (g_taps.transpose(2, 0, 1), g_first.T, g_mid, g_out)


def solution(mesh):
    in_specs = (
        P("dp", "band", None, None),
        P("band", None, None),
        P(),
        P(),
        P(),
        P("dp", None, "band", None),
        P("dp", "band", None),
    )
    out_specs = (P("band", None, None), P(), P(), P())
    return jax.shard_map(
        functools.partial(on_device, mesh.shape["dp"], mesh.shape["band"]),
        mesh=mesh, in_specs=in_specs, out_specs=out_specs, check_vma=False,
    )
```

```python
import functools
import math

import jax
import jax.numpy as jnp
from jax import lax
from jax.experimental import pallas as pl
from jax.experimental.pallas import tpu as pltpu
from jax.sharding import PartitionSpec as P

MESH = pl.DeviceIdType.MESH
F32 = jnp.float32
BF16 = jnp.bfloat16


def up(value, step):
    return -(-value // step) * step


def mm(a, b):
    return jnp.dot(a, b, preferred_element_type=F32)


def mm_tn(a, b):
    return lax.dot_general(a, b, (((0,), (0,)), ((), ())), preferred_element_type=F32)


def eye(n):
    same = lax.broadcasted_iota(jnp.int32, (n, n), 0) == lax.broadcasted_iota(jnp.int32, (n, n), 1)
    return jnp.where(same, 1.0, 0.0).astype(BF16)


def mm_nt(a, b):
    return lax.dot_general(a, b, (((1,), (1,)), ((), ())), preferred_element_type=F32)


def kernel(
    cfg,
    x_ref, taps_ref, w1t_ref, wm_ref, wo_ref, target_ref, mask_ref,
    gk_ref, gf_ref, gm_ref, go_ref,
    tap_rows, taps_own, wft_ref, wf_ref, wmt_ref, wot_ref, wanted, sums, stack, filt, slope, z_send, z_recv, dz_all, hid_s,
    early, early_in, early_x, early_out, first_g, first_in, first_out, late, late_in,
    z_ss, z_rs, d_ss, d_rs, e_ss, e_rs, ex_ss, ex_rs, ea_ss, ea_rs,
    f_ss, f_rs, fa_ss, fa_rs, l_ss, l_rs, la_ss, la_rs,
):
    nd, nb = cfg["nd"], cfg["nb"]
    bands, unroll, bp, ks = cfg["bands"], cfg["unroll"], cfg["bp"], cfg["ks"]
    fs, ts = cfg["fs"], cfg["ts"]
    rows_all, rows, width, chunks = cfg["rows_all"], cfg["rows"], cfg["width"], cfg["chunks"]
    ch, outs, scale = cfg["ch"], cfg["outs"], cfg["scale"]
    ew, gw, lw = cfg["ew"], cfg["gw"], cfg["lw"]
    half = ks // 2
    lanes = 8 * rows_all
    step_rows = rows // chunks
    me_d = lax.axis_index("dp")
    me_b = lax.axis_index("band")
    me = me_d * nb + me_b
    total = nd * nb
    split = nb == 2

    def device(index):
        return (index // nb, lax.rem(index, nb))

    barrier = pltpu.get_barrier_semaphore()

    def greet(k, _):
        pl.semaphore_signal(
            barrier, inc=1, device_id=device(lax.rem(me + k, total)), device_id_type=MESH
        )
        return 0

    lax.fori_loop(1, total, greet, 0)

    row_i = lax.broadcasted_iota(jnp.int32, (rows_all, lanes), 0)
    lane_i = lax.broadcasted_iota(jnp.int32, (rows_all, lanes), 1)
    block = lane_i // rows_all
    tap = lane_i % rows_all - row_i + half
    band_mask = (tap >= 0) & (tap < ks) & (block < ks)
    col = lax.broadcasted_iota(jnp.int32, (rows_all, width), 1)
    for h in range(rows_all):
        filt[pl.ds(h * fs + bp - 16, 16), :] = jnp.zeros((16, width), F32)

    place_j = lax.broadcasted_iota(jnp.int32, (ks, lanes), 0)
    place_l = lax.broadcasted_iota(jnp.int32, (ks, lanes), 1) - (8 - half)
    base = jnp.zeros((bands, lanes), F32)
    for i in range(ks):
        spot = jnp.where(place_l == place_j * rows_all + i, 1.0, 0.0).astype(BF16)
        base = base + mm_tn(taps_ref[i], spot)
    tap_rows[0:bands, :] = base

    lower = me_b == 0
    mid_row = rows_all // 2

    def filter_band(b):
        image = x_ref[b]
        parts = []
        for j in range(ks):
            s = j - half
            if s == 0:
                moved = image
            else:
                moved = pltpu.roll(image, (-s) % width, 1)
                moved = jnp.where((col + s >= 0) & (col + s < width), moved, jnp.zeros((), BF16))
            parts.append(moved)
        parts.append(jnp.zeros((lanes - ks * rows_all, width), BF16))
        moved_all = jnp.concatenate(parts, axis=0)
        stack[b] = moved_all
        spread = jnp.broadcast_to(tap_rows[pl.ds(b, 1), :], (rows_all, lanes))
        taps = pltpu.roll(spread, lanes - 8, 1, stride=1, stride_axis=0)
        taps = jnp.where(band_mask, taps, 0.0)
        if split:
            taps_own[b] = jnp.where(lower, taps[:mid_row], taps[mid_row:]).astype(BF16)
            taps = jnp.where(lower, taps[mid_row:], taps[:mid_row])
            first, count = (1 - me_b) * rows, rows
        else:
            first, count = 0, rows_all
        out = mm(taps.astype(BF16), moved_all)
        filt[pl.ds(first * fs + b, count, stride=fs), :] = out.astype(BF16).astype(F32)

    def filter_own(b):
        out = mm(taps_own[b], stack[b])
        filt[pl.ds(me_b * rows * fs + b, rows, stride=fs), :] = out.astype(BF16).astype(F32)

    def over_bands(lo, hi, act):
        def body(g, _):
            for q in range(unroll):
                act(g * unroll + q)
            return 0

        lax.fori_loop(lo, hi, body, 0)

    groups = bands // unroll
    over_bands(0, groups, filter_band)

    pick = jnp.where(
        lax.broadcasted_iota(jnp.int32, (bp, outs), 1)
        == lax.broadcasted_iota(jnp.int32, (bp, outs), 0) + me_b * bands,
        1.0, 0.0,
    )
    pick = jnp.where(lax.broadcasted_iota(jnp.int32, (bp, outs), 0) < bands, pick, 0.0).astype(BF16)
    wft_ref[...] = mm_nt(w1t_ref[...], pick).astype(BF16)

    def filt_rows(h, count):
        return jnp.concatenate(
            [
                filt[pl.ds(pl.multiple_of((h + r) * fs, 8), bp), :].astype(BF16)
                for r in range(count)
            ],
            axis=1,
        )

    pl.semaphore_wait(barrier, total - 1)

    def z_copy(k, c):
        part = pl.ds(c * step_rows, step_rows)
        return pltpu.make_async_remote_copy(
            src_ref=z_send.at[k, part],
            dst_ref=z_recv.at[k, part],
            send_sem=z_ss.at[k, c],
            recv_sem=z_rs.at[k, c],
            device_id=(me_d, lax.rem(me_b + k, nb)),
            device_id_type=MESH,
        )

    def z_part(k, c):
        owner = lax.rem(me_b + k, nb)

        def one(p, _):
            h = c * step_rows + p * 2
            z = mm(wft_ref[...], filt_rows(owner * rows + h, 2))
            z_send[k, h] = z[:, :width]
            z_send[k, h + 1] = z[:, width:]
            return 0

        lax.fori_loop(0, step_rows // 2, one, 0, unroll=True)

    for k in range(1, nb):
        for c in range(chunks):
            z_part(k, c)
            z_copy(k, c).start()
    if split:
        over_bands(0, groups, filter_own)
    for c in range(chunks):
        z_part(0, c)
    wf_ref[...] = mm_nt(pick, w1t_ref[...]).astype(BF16)
    wmt_ref[...] = mm_nt(eye(ch), wm_ref[...]).astype(BF16)
    wot_ref[...] = mm_nt(eye(outs), wo_ref[...]).astype(BF16)
    if ts == rows:
        wanted[...] = target_ref[...].astype(F32)
    else:
        def widen(g, _):
            for q in range(8):
                o = g * 8 + q
                block_o = target_ref[pl.ds(pl.multiple_of(o * rows, 16), rows), :]
                wanted[pl.ds(pl.multiple_of(o * ts, 8), rows), :] = block_o.astype(F32)
            return 0

        lax.fori_loop(0, outs // 8, widen, 0)

    def d_copy(k, c):
        part = pl.ds(me_b * rows + c * step_rows, step_rows)
        return pltpu.make_async_remote_copy(
            src_ref=dz_all.at[part],
            dst_ref=dz_all.at[part],
            send_sem=d_ss.at[k, c],
            recv_sem=d_rs.at[k, c],
            device_id=(me_d, lax.rem(me_b + k, nb)),
            device_id_type=MESH,
        )

    def wide(pieces):
        return jnp.concatenate(pieces, axis=1)

    g_out = jnp.zeros((ch, outs), F32)
    g_mid = jnp.zeros((ch, ch), F32)
    for c in range(chunks):
        for k in range(1, nb):
            z_copy(k, c).wait_recv()
        z_list = []
        for r in range(step_rows):
            h = c * step_rows + r
            z = z_send[0, h]
            for k in range(1, nb):
                z = z + z_recv[k, h]
            z_list.append(z)
        z_first = wide(z_list)
        sig_first = jax.nn.sigmoid(z_first)
        hid_first = (z_first * sig_first).astype(BF16)
        z_mid = mm(wmt_ref[...], hid_first)
        sig_mid = jax.nn.sigmoid(z_mid)
        hid_mid = (hid_first.astype(F32) + z_mid * sig_mid).astype(BF16)
        predicted = mm(wot_ref[...], hid_mid)
        errs = []
        for r in range(step_rows):
            h = c * step_rows + r
            factor = (2.0 * scale) * mask_ref[pl.ds(h, 1), :].astype(F32)
            diff = predicted[:, r * width:(r + 1) * width] - wanted[pl.ds(h, outs, stride=ts), :]
            errs.append((factor * diff).astype(BF16))
        err = wide(errs)
        g_out = g_out + mm_nt(hid_mid, err)
        d_mid = mm(wo_ref[...], err)
        dz_mid = (d_mid * (sig_mid * (1.0 + z_mid * (1.0 - sig_mid)))).astype(BF16)
        g_mid = g_mid + mm_nt(hid_first, dz_mid)
        d_first = d_mid + mm(wm_ref[...], dz_mid)
        dz = (d_first * (sig_first * (1.0 + z_first * (1.0 - sig_first)))).astype(BF16)
        for r in range(step_rows):
            h = c * step_rows + r
            dz_all[me_b * rows + h] = dz[:, r * width:(r + 1) * width]
        for k in range(1, nb):
            d_copy(k, c).start()

    def piece(ref, index, w):
        lane_parts = nd // 8
        each_w = w // lane_parts
        return ref.at[
            pl.ds(pl.multiple_of((index // lane_parts) * 8, 8), 8),
            pl.ds(pl.multiple_of(lax.rem(index, lane_parts) * each_w, 128), each_w),
        ]

    def scatter_copy(ref, into, w, ss, rs, k):
        peer = lax.rem(me_d + k, nd)
        return pltpu.make_async_remote_copy(
            src_ref=piece(ref, peer, w),
            dst_ref=into.at[k],
            send_sem=ss.at[k],
            recv_sem=rs.at[k],
            device_id=(peer, me_b),
            device_id_type=MESH,
        )

    def gather_copy(ref, w, ss, rs, device_of, k):
        part = piece(ref, me_d, w)
        return pltpu.make_async_remote_copy(
            src_ref=part,
            dst_ref=part,
            send_sem=ss.at[k],
            recv_sem=rs.at[k],
            device_id=device_of(k),
            device_id_type=MESH,
        )

    def each(count, act):
        def body(k, _):
            act(k)
            return 0

        lax.fori_loop(1, count, body, 0)

    def crop_peer(k):
        return (lax.rem(me_d + k, nd), me_b)

    def any_peer(k):
        return device(lax.rem(me + k, total))

    def add_up(ref, into, w):
        own = piece(ref, me_d, w)[...]
        for k in range(1, nd):
            own = own + into[k]
        return own

    def scatter_early(k):
        return scatter_copy(early, early_in, ew, e_ss, e_rs, k)

    def band_early(k):
        return pltpu.make_async_remote_copy(
            src_ref=early_x.at[0],
            dst_ref=early_x.at[k],
            send_sem=ex_ss.at[k],
            recv_sem=ex_rs.at[k],
            device_id=(me_d, lax.rem(me_b + k, nb)),
            device_id_type=MESH,
        )

    def gather_early(k):
        return gather_copy(early_out, ew, ea_ss, ea_rs, crop_peer, k)

    def scatter_first(k):
        return scatter_copy(first_g, first_in, gw, f_ss, f_rs, k)

    def gather_first(k):
        return gather_copy(first_out.at[me_b], gw, fa_ss, fa_rs, any_peer, k)

    def scatter_late(k):
        return scatter_copy(late, late_in, lw, l_ss, l_rs, k)

    def gather_late(k):
        return gather_copy(gk_ref, lw, la_ss, la_rs, crop_peer, k)

    early[...] = jnp.zeros_like(early)
    early[:, 0:outs] = g_out
    early[:, outs:outs + ch] = g_mid
    each(nd, lambda k: scatter_early(k).start())
    first_g[...] = jnp.zeros_like(first_g)
    late[...] = jnp.zeros_like(late)
    sums[...] = jnp.zeros_like(sums)

    hid_s[...] = jnp.zeros_like(hid_s)

    def slope_rows(first):
        def one(p, _):
            h = first + 2 * p
            dz = wide([dz_all[h], dz_all[h + 1]])
            hid_s[...] += mm_nt(dz, filt_rows(h, 2))
            back = mm(wf_ref[...], dz)
            for r in range(2):
                place = pl.multiple_of((rows_all - 1 - h - r) * fs, 8)
                slope[pl.ds(place, bp), :] = back[:, r * width:(r + 1) * width]
            return 0

        lax.fori_loop(0, step_rows // 2, one, 0, unroll=True)

    skew = lanes - (rows_all - 1) + half
    extra = -skew % 8

    def taps_part(part, start, count, lo, hi):
        lane = lax.broadcasted_iota(jnp.int32, (count, lanes), 1)
        row = lax.broadcasted_iota(jnp.int32, (count, lanes), 0)
        lane = lax.rem(lane + start + (lanes - extra), lanes)
        tap_e = lane % rows_all
        source = rows_all - 1 - start - row + tap_e - half
        valid = (lane < ks * rows_all) & (tap_e < ks) & (source >= 0) & (source < rows_all)

        def taps_band(b):
            rows_b = slope[pl.ds(start * fs + b, count, stride=fs), :].astype(BF16)
            cross = mm_nt(rows_b, stack[b])
            moved = pltpu.roll(cross, (skew + extra) % lanes, 1, stride=1, stride_axis=0)
            moved = jnp.where(valid, moved, 0.0)
            sums[part, pl.ds(b, 1), :] = jnp.sum(moved, axis=0, keepdims=True)

        over_bands(lo, hi, taps_band)

    for c in range(chunks):
        slope_rows(me_b * rows + c * step_rows)
    if split:
        taps_part(0, (1 - me_b) * rows, rows, 0, groups)

    each(nd, lambda k: scatter_early(k).wait_recv())
    early_x[0] = add_up(early, early_in, ew)
    for k in range(1, nb):
        band_early(k).start()

    for k in range(1, nb):
        source = lax.rem(me_b + nb - k, nb)
        for c in range(chunks):
            d_copy(k, c).wait_recv()
            slope_rows(source * rows + c * step_rows)

    first_g[:, 0:bp] = hid_s[...]
    each(nd, lambda k: scatter_first(k).start())
    own = early_x[0]
    for k in range(1, nb):
        band_early(k).wait_recv()
        own = own + early_x[k]
    piece(early_out, me_d, ew)[...] = own
    each(nd, lambda k: gather_early(k).start())

    rest = (me_b * rows, rows) if split else (0, rows_all)
    cut = groups // 2
    taps_part(1, *rest, 0, cut)

    each(nd, lambda k: scatter_first(k).wait_recv())
    piece(first_out.at[me_b], me_d, gw)[...] = add_up(first_g, first_in, gw)
    each(total, lambda k: gather_first(k).start())

    taps_part(1, *rest, cut, groups)

    def pick_taps(part, start):
        slot = (8 * ks, lanes)
        r = lax.broadcasted_iota(jnp.int32, slot, 0)
        lane = lax.broadcasted_iota(jnp.int32, slot, 1)
        lane = lax.rem(lane + start + (lanes - extra), lanes)
        spot = jnp.where(lane == (r % 8) * rows_all + r // 8, 1.0, 0.0)
        return lax.dot_general(
            spot, sums[part], (((1,), (1,)), ((), ())),
            preferred_element_type=F32, precision=lax.Precision.HIGHEST,
        )

    taps_sum = pick_taps(1, rest[0])
    if split:
        taps_sum = taps_sum + pick_taps(0, (1 - me_b) * rows)
    late[0:8 * ks, 0:bp] = taps_sum
    each(nd, lambda k: scatter_late(k).start())

    each(nd, lambda k: gather_early(k).wait_recv())
    go_ref[...] = early_out[:, 0:outs]
    gm_ref[...] = early_out[:, outs:outs + ch]

    each(nd, lambda k: scatter_late(k).wait_recv())
    piece(gk_ref, me_d, lw)[...] = add_up(late, late_in, lw)
    each(nd, lambda k: gather_late(k).start())

    each(total, lambda k: gather_first(k).wait_recv())
    for k in range(nb):
        gf_ref[:, k * bands:(k + 1) * bands] = first_out[k, :, 0:bands]
    each(nd, lambda k: gather_late(k).wait_recv())

    for k in range(1, nb):
        band_early(k).wait_send()
        for c in range(chunks):
            z_copy(k, c).wait_send()
            d_copy(k, c).wait_send()
    each(nd, lambda k: scatter_early(k).wait_send())
    each(nd, lambda k: gather_early(k).wait_send())
    each(nd, lambda k: scatter_first(k).wait_send())
    each(total, lambda k: gather_first(k).wait_send())
    each(nd, lambda k: scatter_late(k).wait_send())
    each(nd, lambda k: gather_late(k).wait_send())


def finish(gk_in, gf_in, gm_in, go_in, gk_out, gf_out, gm_out, go_out):
    ks, _, bands = gk_out.shape
    for i in range(ks):
        gk_out[i] = gk_in[8 * i:8 * i + ks, 0:bands]
    gf_out[...] = gf_in[...]
    gm_out[...] = gm_in[...]
    go_out[...] = go_in[...]


def on_device(nd, nb, radiance, kernel_taps, w_first, w_mid, w_out, target, mask):
    image = radiance[0]
    bands, rows_all, width = image.shape
    ks = kernel_taps.shape[1]
    ch = w_first.shape[1]
    outs = w_out.shape[1]
    rows = rows_all // nb
    chunks = min(4, rows // 2)
    unroll = max(u for u in range(1, 11) if bands % u == 0)
    bp = up(bands, 16)
    fs = bp + 8
    ts = rows + 8 if rows % 16 == 0 and outs % 8 == 0 else rows
    lane_parts = nd // 8
    lanes = 8 * rows_all
    ew = up(outs + ch, 128 * lane_parts)
    gw = up(bp, 128 * lane_parts)
    lw = up(bp, 128 * lane_parts)
    cfg = dict(
        nd=nd, nb=nb, bands=bands, unroll=unroll, bp=bp, ks=ks, rows_all=rows_all, rows=rows,
        width=width, chunks=chunks, ch=ch, outs=outs, ew=ew, gw=gw, lw=lw, fs=fs, ts=ts,
        scale=1.0 / math.sqrt(nd * rows_all * width),
    )
    sems = lambda *shape: pltpu.SemaphoreType.DMA(shape)
    vmem = pl.BlockSpec(memory_space=pltpu.VMEM)
    sums = pl.pallas_call(
        functools.partial(kernel, cfg),
        out_shape=(
            jax.ShapeDtypeStruct((64, lw), F32),
            jax.ShapeDtypeStruct((ch, bands * nb), F32),
            jax.ShapeDtypeStruct((ch, ch), F32),
            jax.ShapeDtypeStruct((ch, outs), F32),
        ),
        in_specs=[vmem] * 7,
        out_specs=(vmem,) * 4,
        scratch_shapes=[
            pltpu.VMEM((bp, lanes), F32),
            pltpu.VMEM((bands, rows_all // 2, lanes), BF16),
            pltpu.VMEM((ch, bp), BF16),
            pltpu.VMEM((bp, ch), BF16),
            pltpu.VMEM((ch, ch), BF16),
            pltpu.VMEM((outs, ch), BF16),
            pltpu.VMEM((outs * ts, width), F32),
            pltpu.VMEM((2, bp, lanes), F32),
            pltpu.VMEM((bands, lanes, width), BF16),
            pltpu.VMEM((rows_all * fs, width), F32),
            pltpu.VMEM((rows_all * fs, width), F32),
            pltpu.VMEM((nb, rows, ch, width), F32),
            pltpu.VMEM((nb, rows, ch, width), F32),
            pltpu.VMEM((rows_all, ch, width), BF16),
            pltpu.VMEM((ch, bp), F32),
            pltpu.VMEM((64, ew), F32),
            pltpu.VMEM((nd, 8, ew // lane_parts), F32),
            pltpu.VMEM((nb, 8, ew // lane_parts), F32),
            pltpu.VMEM((64, ew), F32),
            pltpu.VMEM((64, gw), F32),
            pltpu.VMEM((nd, 8, gw // lane_parts), F32),
            pltpu.VMEM((nb, 64, gw), F32),
            pltpu.VMEM((64, lw), F32),
            pltpu.VMEM((nd, 8, lw // lane_parts), F32),
            sems(nb, chunks), sems(nb, chunks), sems(nb, chunks), sems(nb, chunks),
            sems(nd), sems(nd), sems(nb), sems(nb), sems(nd), sems(nd),
            sems(nd), sems(nd), sems(nd * nb), sems(nd * nb),
            sems(nd), sems(nd), sems(nd), sems(nd),
        ],
        compiler_params=pltpu.CompilerParams(
            collective_id=0, has_side_effects=True, vmem_limit_bytes=56 * 1024 * 1024
        ),
    )(
        image, kernel_taps.transpose(1, 2, 0), w_first.T, w_mid, w_out,
        target[0].reshape(outs * rows, width), mask[0],
    )
    g_taps, g_first, g_mid, g_out = pl.pallas_call(
        finish,
        out_shape=(
            jax.ShapeDtypeStruct((ks, ks, bands), F32),
            jax.ShapeDtypeStruct((ch, bands * nb), F32),
            jax.ShapeDtypeStruct((ch, ch), F32),
            jax.ShapeDtypeStruct((ch, outs), F32),
        ),
        in_specs=[vmem] * 4,
        out_specs=(vmem,) * 4,
    )(*sums)
    return (g_taps.transpose(2, 0, 1), g_first.T, g_mid, g_out)


def solution(mesh):
    in_specs = (
        P("dp", "band", None, None),
        P("band", None, None),
        P(),
        P(),
        P(),
        P("dp", None, "band", None),
        P("dp", "band", None),
    )
    out_specs = (P("band", None, None), P(), P(), P())
    return jax.shard_map(
        functools.partial(on_device, mesh.shape["dp"], mesh.shape["band"]),
        mesh=mesh, in_specs=in_specs, out_specs=out_specs, check_vma=False,
    )
```

```python
import functools
import math

import jax
import jax.numpy as jnp
from jax import lax
from jax.experimental import pallas as pl
from jax.experimental.pallas import tpu as pltpu
from jax.sharding import PartitionSpec as P

MESH = pl.DeviceIdType.MESH
F32 = jnp.float32
BF16 = jnp.bfloat16


def up(value, step):
    return -(-value // step) * step


def mm(a, b):
    return jnp.dot(a, b, preferred_element_type=F32)


def mm_tn(a, b):
    return lax.dot_general(a, b, (((0,), (0,)), ((), ())), preferred_element_type=F32)


def eye(n):
    same = lax.broadcasted_iota(jnp.int32, (n, n), 0) == lax.broadcasted_iota(jnp.int32, (n, n), 1)
    return jnp.where(same, 1.0, 0.0).astype(BF16)


def mm_nt(a, b):
    return lax.dot_general(a, b, (((1,), (1,)), ((), ())), preferred_element_type=F32)


def kernel(
    cfg,
    x_ref, taps_ref, w1t_ref, wm_ref, wo_ref, target_ref, mask_ref,
    gk_ref, gf_ref, gm_ref, go_ref,
    band_mask, edge, diag_mask, tap_rows, taps_own, wft_ref, wf_ref, wmt_ref, wot_ref, wanted, sums, stack, filt, slope, z_send, z_recv, dz_all, hid_s,
    early, early_in, early_out, total_ref, sides, late, late_in, late_out,
    z_ss, z_rs, d_ss, d_rs, ex_ss, ex_rs, e_ss, e_rs, ea_ss, ea_rs, l_ss, l_rs, la_ss, la_rs,
):
    nd, nb = cfg["nd"], cfg["nb"]
    bands, unroll, bp, ks = cfg["bands"], cfg["unroll"], cfg["bp"], cfg["ks"]
    fs, ts = cfg["fs"], cfg["ts"]
    rows_all, rows, width, chunks = cfg["rows_all"], cfg["rows"], cfg["width"], cfg["chunks"]
    ch, outs, scale = cfg["ch"], cfg["outs"], cfg["scale"]
    ew, lw = cfg["ew"], cfg["lw"]
    half = ks // 2
    lanes = 8 * rows_all
    step_rows = rows // chunks
    me_d = lax.axis_index("dp")
    me_b = lax.axis_index("band")
    split = nb == 2

    def each(count, act):
        if count <= 16:
            for k in range(1, count):
                act(k)
            return

        def body(k, _):
            act(k)
            return 0

        lax.fori_loop(1, count, body, 0)

    def crop_peer(k):
        return (lax.rem(me_d + k, nd), me_b)

    def band_peer(k):
        return (me_d, lax.rem(me_b + k, nb))

    barrier = pltpu.get_barrier_semaphore()

    def greet(peer):
        pl.semaphore_signal(barrier, inc=1, device_id=peer, device_id_type=MESH)

    each(nd, lambda k: greet(crop_peer(k)))
    each(nb, lambda k: greet(band_peer(k)))

    row_i = lax.broadcasted_iota(jnp.int32, (rows_all, lanes), 0)
    lane_i = lax.broadcasted_iota(jnp.int32, (rows_all, lanes), 1)
    block = lane_i // rows_all
    tap = lane_i % rows_all - row_i + half
    band_mask[...] = jnp.where((tap >= 0) & (tap < ks) & (block < ks), 1.0, 0.0)
    col = lax.broadcasted_iota(jnp.int32, (rows_all, width), 1)
    for j in range(ks):
        inside = (col + (j - half) >= 0) & (col + (j - half) < width)
        edge[j] = jnp.where(inside, 1.0, 0.0).astype(BF16)
    for h in range(rows_all):
        filt[pl.ds(h * fs + bp - 16, 16), :] = jnp.zeros((16, width), F32)

    place_j = lax.broadcasted_iota(jnp.int32, (ks, lanes), 0)
    place_l = lax.broadcasted_iota(jnp.int32, (ks, lanes), 1) - (8 - half)
    base = jnp.zeros((bands, lanes), F32)
    for i in range(ks):
        spot = jnp.where(place_l == place_j * rows_all + i, 1.0, 0.0).astype(BF16)
        base = base + mm_tn(taps_ref[i], spot)
    tap_rows[0:bands, :] = base

    lower = me_b == 0
    mid_row = rows_all // 2

    def filter_band(b):
        image = x_ref[b]
        parts = []
        for j in range(ks):
            s = j - half
            if s == 0:
                moved = image
            else:
                moved = pltpu.roll(image, (-s) % width, 1) * edge[j]
            parts.append(moved)
        parts.append(jnp.zeros((lanes - ks * rows_all, width), BF16))
        moved_all = jnp.concatenate(parts, axis=0)
        stack[b] = moved_all
        spread = jnp.broadcast_to(tap_rows[pl.ds(b, 1), :], (rows_all, lanes))
        taps = pltpu.roll(spread, lanes - 8, 1, stride=1, stride_axis=0)
        taps = taps * band_mask[...]
        if split:
            taps_own[b] = jnp.where(lower, taps[:mid_row], taps[mid_row:]).astype(BF16)
            taps = jnp.where(lower, taps[mid_row:], taps[:mid_row])
            first, count = (1 - me_b) * rows, rows
        else:
            first, count = 0, rows_all
        out = mm(taps.astype(BF16), moved_all)
        filt[pl.ds(first * fs + b, count, stride=fs), :] = out.astype(BF16).astype(F32)

    def filter_own(b):
        out = mm(taps_own[b], stack[b])
        filt[pl.ds(me_b * rows * fs + b, rows, stride=fs), :] = out.astype(BF16).astype(F32)

    def over_bands(lo, hi, act):
        def body(g, _):
            for q in range(unroll):
                act(g * unroll + q)
            return 0

        lax.fori_loop(lo, hi, body, 0)

    groups = bands // unroll
    over_bands(0, groups, filter_band)

    pick = jnp.where(
        lax.broadcasted_iota(jnp.int32, (bp, outs), 1)
        == lax.broadcasted_iota(jnp.int32, (bp, outs), 0) + me_b * bands,
        1.0, 0.0,
    )
    pick = jnp.where(lax.broadcasted_iota(jnp.int32, (bp, outs), 0) < bands, pick, 0.0).astype(BF16)
    wft_ref[...] = mm_nt(w1t_ref[...], pick).astype(BF16)

    def filt_rows(h, count):
        return jnp.concatenate(
            [
                filt[pl.ds(pl.multiple_of((h + r) * fs, 8), bp), :].astype(BF16)
                for r in range(count)
            ],
            axis=1,
        )

    pl.semaphore_wait(barrier, nd + nb - 2)

    def z_copy(k, c):
        part = pl.ds(c * step_rows, step_rows)
        return pltpu.make_async_remote_copy(
            src_ref=z_send.at[k, part],
            dst_ref=z_recv.at[k, part],
            send_sem=z_ss.at[k, c],
            recv_sem=z_rs.at[k, c],
            device_id=(me_d, lax.rem(me_b + k, nb)),
            device_id_type=MESH,
        )

    def z_part(k, c):
        owner = lax.rem(me_b + k, nb)

        def one(p, _):
            h = c * step_rows + p * 2
            z = mm(wft_ref[...], filt_rows(owner * rows + h, 2))
            z_send[k, h] = z[:, :width]
            z_send[k, h + 1] = z[:, width:]
            return 0

        lax.fori_loop(0, step_rows // 2, one, 0, unroll=True)

    for k in range(1, nb):
        for c in range(chunks):
            z_part(k, c)
            z_copy(k, c).start()
    if split:
        over_bands(0, groups, filter_own)
    for c in range(chunks):
        z_part(0, c)
    wf_ref[...] = mm_nt(pick, w1t_ref[...]).astype(BF16)
    wmt_ref[...] = mm_nt(eye(ch), wm_ref[...]).astype(BF16)
    wot_ref[...] = mm_nt(eye(outs), wo_ref[...]).astype(BF16)
    if ts == rows:
        wanted[...] = target_ref[...].astype(F32)
    else:
        def widen(g, _):
            for q in range(8):
                o = g * 8 + q
                block_o = target_ref[pl.ds(pl.multiple_of(o * rows, 16), rows), :]
                wanted[pl.ds(pl.multiple_of(o * ts, 8), rows), :] = block_o.astype(F32)
            return 0

        lax.fori_loop(0, outs // 8, widen, 0)

    def d_copy(k, c):
        part = pl.ds(me_b * rows + c * step_rows, step_rows)
        return pltpu.make_async_remote_copy(
            src_ref=dz_all.at[part],
            dst_ref=dz_all.at[part],
            send_sem=d_ss.at[k, c],
            recv_sem=d_rs.at[k, c],
            device_id=(me_d, lax.rem(me_b + k, nb)),
            device_id_type=MESH,
        )

    def wide(pieces):
        return jnp.concatenate(pieces, axis=1)

    g_out = jnp.zeros((ch, outs), F32)
    g_mid = jnp.zeros((ch, ch), F32)
    for c in range(chunks):
        for k in range(1, nb):
            z_copy(k, c).wait_recv()
        z_list = []
        for r in range(step_rows):
            h = c * step_rows + r
            z = z_send[0, h]
            for k in range(1, nb):
                z = z + z_recv[k, h]
            z_list.append(z)
        z_first = wide(z_list)
        sig_first = jax.nn.sigmoid(z_first)
        hid_first = (z_first * sig_first).astype(BF16)
        z_mid = mm(wmt_ref[...], hid_first)
        sig_mid = jax.nn.sigmoid(z_mid)
        hid_mid = (hid_first.astype(F32) + z_mid * sig_mid).astype(BF16)
        predicted = mm(wot_ref[...], hid_mid)
        errs = []
        for r in range(step_rows):
            h = c * step_rows + r
            factor = (2.0 * scale) * mask_ref[pl.ds(h, 1), :].astype(F32)
            diff = predicted[:, r * width:(r + 1) * width] - wanted[pl.ds(h, outs, stride=ts), :]
            errs.append((factor * diff).astype(BF16))
        err = wide(errs)
        g_out = g_out + mm_nt(hid_mid, err)
        d_mid = mm(wo_ref[...], err)
        dz_mid = (d_mid * (sig_mid * (1.0 + z_mid * (1.0 - sig_mid)))).astype(BF16)
        g_mid = g_mid + mm_nt(hid_first, dz_mid)
        d_first = d_mid + mm(wm_ref[...], dz_mid)
        dz = (d_first * (sig_first * (1.0 + z_first * (1.0 - sig_first)))).astype(BF16)
        for r in range(step_rows):
            h = c * step_rows + r
            dz_all[me_b * rows + h] = dz[:, r * width:(r + 1) * width]
        for k in range(1, nb):
            d_copy(k, c).start()

    def piece(ref, index, w):
        lane_parts = nd // 8
        each_w = w // lane_parts
        return ref.at[
            pl.ds(pl.multiple_of((index // lane_parts) * 8, 8), 8),
            pl.ds(pl.multiple_of(lax.rem(index, lane_parts) * each_w, 128), each_w),
        ]

    def remote(src, dst, ss, rs, peer):
        return pltpu.make_async_remote_copy(
            src_ref=src, dst_ref=dst, send_sem=ss, recv_sem=rs,
            device_id=peer, device_id_type=MESH,
        )

    def scatter(ref, into, w, ss, rs):
        def start(k):
            peer = crop_peer(k)
            remote(piece(ref, peer[0], w), into.at[k], ss, rs, peer).start()

        each(nd, start)

    def gather(out, ss, rs):
        def start(k):
            remote(out.at[me_d], out.at[me_d], ss, rs, crop_peer(k)).start()

        each(nd, start)

    def wait_all(ref, sem):
        rest = ref.at[pl.ds(1, nd - 1)]
        pltpu.make_async_copy(rest, rest, sem).wait()

    def add_up(ref, into, w):
        own = piece(ref, me_d, w)[...]
        for k in range(1, nd):
            own = own + into[k]
        return own

    def band_early(k):
        return remote(
            early_out.at[me_d, me_b], early_out.at[me_d, me_b], ex_ss.at[k], ex_rs.at[k], band_peer(k)
        )

    def spread_out(out, w, put):
        lane_parts = nd // 8
        each_w = w // lane_parts
        for d in range(nd):
            put(out, d, (d // lane_parts) * 8, (d % lane_parts) * each_w, each_w)

    early[...] = jnp.zeros_like(early)
    late[...] = jnp.zeros_like(late)
    sums[...] = jnp.zeros_like(sums)

    hid_s[...] = jnp.zeros_like(hid_s)

    def slope_rows(first):
        def one(p, _):
            h = first + 2 * p
            dz = wide([dz_all[h], dz_all[h + 1]])
            hid_s[...] += mm_nt(dz, filt_rows(h, 2))
            back = mm(wf_ref[...], dz)
            for r in range(2):
                place = pl.multiple_of((rows_all - 1 - h - r) * fs, 8)
                slope[pl.ds(place, bp), :] = back[:, r * width:(r + 1) * width]
            return 0

        lax.fori_loop(0, step_rows // 2, one, 0, unroll=True)

    skew = lanes - (rows_all - 1) + half
    extra = -skew % 8

    lane = lax.rem(lane_i + (lanes - extra), lanes)
    tap_e = lane % rows_all
    source_e = rows_all - 1 - row_i + tap_e - half
    valid = (lane < ks * rows_all) & (tap_e < ks) & (source_e >= 0) & (source_e < rows_all)
    diag_mask[...] = jnp.where(valid, 1.0, 0.0)

    def taps_band(b):
        rows_b = slope[pl.ds(b, rows_all, stride=fs), :].astype(BF16)
        cross = mm_nt(rows_b, stack[b])
        moved = pltpu.roll(cross, (skew + extra) % lanes, 1, stride=1, stride_axis=0)
        moved = moved * diag_mask[...]
        acc = moved[0:8]
        for r in range(8, rows_all, 8):
            acc = acc + moved[r:r + 8]
        for part in range(lanes // 128):
            sums[part, pl.ds(pl.multiple_of(b * 8, 8), 8), :] = acc[:, part * 128:(part + 1) * 128]

    for c in range(chunks):
        slope_rows(me_b * rows + c * step_rows)
    for k in range(1, nb):
        source = lax.rem(me_b + nb - k, nb)
        for c in range(chunks):
            d_copy(k, c).wait_recv()
            slope_rows(source * rows + c * step_rows)

    early[:, 0:outs] = g_out
    early[:, outs:outs + ch] = g_mid
    early[:, outs + ch:outs + ch + bands] = hid_s[:, 0:bands]
    scatter(early, early_in, ew, e_ss, e_rs)

    first, second = groups * 2 // 5, groups * 7 // 10
    over_bands(0, first, taps_band)

    wait_all(early_in, e_rs)
    early_out[me_d, me_b] = add_up(early, early_in, ew)
    for k in range(1, nb):
        band_early(k).start()

    over_bands(first, second, taps_band)

    for k in range(1, nb):
        band_early(k).wait_recv()
    gather(early_out, ea_ss, ea_rs)

    over_bands(second, groups, taps_band)

    slot_r = lax.broadcasted_iota(jnp.int32, (8 * ks, lanes), 0)
    slot_l = lax.broadcasted_iota(jnp.int32, (8 * ks, lanes), 1) - extra
    spot = jnp.where(slot_l == (slot_r % 8) * rows_all + slot_r // 8, 1.0, 0.0)
    parts = []
    for part in range(lanes // 128):
        rows_sum = sums[part, pl.ds(0, bp, stride=8), :]
        for r in range(1, 8):
            rows_sum = rows_sum + sums[part, pl.ds(r, bp, stride=8), :]
        parts.append(rows_sum)
    per_band = wide(parts)
    late[0:8 * ks, 0:bp] = lax.dot_general(
        spot, per_band, (((1,), (1,)), ((), ())),
        preferred_element_type=F32, precision=lax.Precision.HIGHEST,
    )
    scatter(late, late_in, lw, l_ss, l_rs)

    wait_all(early_out, ea_rs)

    def put_early(out, d, r, w0, w):
        both = out[d, 0]
        for k in range(1, nb):
            both = both + out[d, k]
        total_ref[r:r + 8, w0:w0 + w] = both
        for k in range(nb):
            sides[k, r:r + 8, w0:w0 + w] = out[d, k]

    spread_out(early_out, ew, put_early)
    go_ref[...] = total_ref[:, 0:outs]
    gm_ref[...] = total_ref[:, outs:outs + ch]
    for k in range(nb):
        gf_ref[:, k * bands:(k + 1) * bands] = sides[k, :, outs + ch:outs + ch + bands]

    wait_all(late_in, l_rs)
    late_out[me_d] = add_up(late, late_in, lw)
    gather(late_out, la_ss, la_rs)
    for k in range(1, nb):
        band_early(k).wait_send()
        for c in range(chunks):
            z_copy(k, c).wait_send()
            d_copy(k, c).wait_send()
    wait_all(early_in, e_ss)
    wait_all(early_out, ea_ss)
    wait_all(late_in, l_ss)
    wait_all(late_out, la_rs)

    def put_late(out, d, r, w0, w):
        gk_ref[r:r + 8, w0:w0 + w] = out[d]

    spread_out(late_out, lw, put_late)
    wait_all(late_out, la_ss)


def finish(gk_in, gf_in, gm_in, go_in, gk_out, gf_out, gm_out, go_out):
    ks, _, bands = gk_out.shape
    for i in range(ks):
        gk_out[i] = gk_in[8 * i:8 * i + ks, 0:bands]
    gf_out[...] = gf_in[...]
    gm_out[...] = gm_in[...]
    go_out[...] = go_in[...]


def on_device(nd, nb, radiance, kernel_taps, w_first, w_mid, w_out, target, mask):
    image = radiance[0]
    bands, rows_all, width = image.shape
    ks = kernel_taps.shape[1]
    ch = w_first.shape[1]
    outs = w_out.shape[1]
    rows = rows_all // nb
    chunks = min(4, rows // 2)
    unroll = max(u for u in range(1, 11) if bands % u == 0)
    bp = up(bands, 16)
    fs = bp + 8
    ts = rows + 8 if rows % 16 == 0 and outs % 8 == 0 else rows
    lane_parts = nd // 8
    lanes = 8 * rows_all
    ew = up(outs + ch + bands, 128 * lane_parts)
    lw = up(bp, 128 * lane_parts)
    cfg = dict(
        nd=nd, nb=nb, bands=bands, unroll=unroll, bp=bp, ks=ks, rows_all=rows_all, rows=rows,
        width=width, chunks=chunks, ch=ch, outs=outs, ew=ew, lw=lw, fs=fs, ts=ts,
        scale=1.0 / math.sqrt(nd * rows_all * width),
    )
    sems = lambda *shape: pltpu.SemaphoreType.DMA(shape)
    vmem = pl.BlockSpec(memory_space=pltpu.VMEM)
    sums = pl.pallas_call(
        functools.partial(kernel, cfg),
        out_shape=(
            jax.ShapeDtypeStruct((64, lw), F32),
            jax.ShapeDtypeStruct((ch, bands * nb), F32),
            jax.ShapeDtypeStruct((ch, ch), F32),
            jax.ShapeDtypeStruct((ch, outs), F32),
        ),
        in_specs=[vmem] * 7,
        out_specs=(vmem,) * 4,
        scratch_shapes=[
            pltpu.VMEM((rows_all, lanes), F32),
            pltpu.VMEM((ks, rows_all, width), BF16),
            pltpu.VMEM((rows_all, lanes), F32),
            pltpu.VMEM((bp, lanes), F32),
            pltpu.VMEM((bands, rows_all // 2, lanes), BF16),
            pltpu.VMEM((ch, bp), BF16),
            pltpu.VMEM((bp, ch), BF16),
            pltpu.VMEM((ch, ch), BF16),
            pltpu.VMEM((outs, ch), BF16),
            pltpu.VMEM((outs * ts, width), F32),
            pltpu.VMEM((lanes // 128, 8 * bp, 128), F32),
            pltpu.VMEM((bands, lanes, width), BF16),
            pltpu.VMEM((rows_all * fs, width), F32),
            pltpu.VMEM((rows_all * fs, width), F32),
            pltpu.VMEM((nb, rows, ch, width), F32),
            pltpu.VMEM((nb, rows, ch, width), F32),
            pltpu.VMEM((rows_all, ch, width), BF16),
            pltpu.VMEM((ch, bp), F32),
            pltpu.VMEM((64, ew), F32),
            pltpu.VMEM((nd, 8, ew // lane_parts), F32),
            pltpu.VMEM((nd, nb, 8, ew // lane_parts), F32),
            pltpu.VMEM((64, ew), F32),
            pltpu.VMEM((nb, 64, ew), F32),
            pltpu.VMEM((64, lw), F32),
            pltpu.VMEM((nd, 8, lw // lane_parts), F32),
            pltpu.VMEM((nd, 8, lw // lane_parts), F32),
            sems(nb, chunks), sems(nb, chunks), sems(nb, chunks), sems(nb, chunks),
            sems(nb), sems(nb), *[pltpu.SemaphoreType.DMA] * 8,
        ],
        compiler_params=pltpu.CompilerParams(
            collective_id=0, has_side_effects=True, vmem_limit_bytes=56 * 1024 * 1024
        ),
    )(
        image, kernel_taps.transpose(1, 2, 0), w_first.T, w_mid, w_out,
        target[0].reshape(outs * rows, width), mask[0],
    )
    g_taps, g_first, g_mid, g_out = pl.pallas_call(
        finish,
        out_shape=(
            jax.ShapeDtypeStruct((ks, ks, bands), F32),
            jax.ShapeDtypeStruct((ch, bands * nb), F32),
            jax.ShapeDtypeStruct((ch, ch), F32),
            jax.ShapeDtypeStruct((ch, outs), F32),
        ),
        in_specs=[vmem] * 4,
        out_specs=(vmem,) * 4,
    )(*sums)
    return (g_taps.transpose(2, 0, 1), g_first.T, g_mid, g_out)


def solution(mesh):
    in_specs = (
        P("dp", "band", None, None),
        P("band", None, None),
        P(),
        P(),
        P(),
        P("dp", None, "band", None),
        P("dp", "band", None),
    )
    out_specs = (P("band", None, None), P(), P(), P())
    return jax.shard_map(
        functools.partial(on_device, mesh.shape["dp"], mesh.shape["band"]),
        mesh=mesh, in_specs=in_specs, out_specs=out_specs, check_vma=False,
    )
```

```python
import functools
import math

import jax
import jax.numpy as jnp
from jax import lax
from jax.experimental import pallas as pl
from jax.experimental.pallas import tpu as pltpu
from jax.sharding import PartitionSpec as P

MESH = pl.DeviceIdType.MESH
F32 = jnp.float32
BF16 = jnp.bfloat16


def up(value, step):
    return -(-value // step) * step


def mm(a, b):
    return jnp.dot(a, b, preferred_element_type=F32)


def mm_tn(a, b):
    return lax.dot_general(a, b, (((0,), (0,)), ((), ())), preferred_element_type=F32)


def eye(n):
    same = lax.broadcasted_iota(jnp.int32, (n, n), 0) == lax.broadcasted_iota(jnp.int32, (n, n), 1)
    return jnp.where(same, 1.0, 0.0).astype(BF16)


def mm_nt(a, b):
    return lax.dot_general(a, b, (((1,), (1,)), ((), ())), preferred_element_type=F32)


def kernel(
    cfg,
    x_ref, taps_ref, w1t_ref, wm_ref, wo_ref, target_ref, mask_ref,
    gk_ref, gf_ref, gm_ref, go_ref,
    band_mask, edge, diag_mask, tap_rows, taps_all, wft_ref, wf_ref, wmt_ref, wot_ref, wanted, sums, stack, filt, slope, z_send, z_recv, dz_all, hid_s,
    early, early_in, early_out, total_ref, sides, late, late_in, late_out,
    z_ss, z_rs, d_ss, d_rs, ex_ss, ex_rs, e_ss, e_rs, ea_ss, ea_rs, l_ss, l_rs, la_ss, la_rs,
):
    nd, nb = cfg["nd"], cfg["nb"]
    bands, unroll, bp, ks = cfg["bands"], cfg["unroll"], cfg["bp"], cfg["ks"]
    fs, ts = cfg["fs"], cfg["ts"]
    rows_all, rows, width, chunks = cfg["rows_all"], cfg["rows"], cfg["width"], cfg["chunks"]
    ch, outs, scale = cfg["ch"], cfg["outs"], cfg["scale"]
    ew, lw = cfg["ew"], cfg["lw"]
    half = ks // 2
    lanes = 8 * rows_all
    step_rows = rows // chunks
    me_d = lax.axis_index("dp")
    me_b = lax.axis_index("band")
    split = nb == 2

    def each(count, act):
        if count <= 16:
            for k in range(1, count):
                act(k)
            return

        def body(k, _):
            act(k)
            return 0

        lax.fori_loop(1, count, body, 0)

    def crop_peer(k):
        return (lax.rem(me_d + k, nd), me_b)

    def band_peer(k):
        return (me_d, lax.rem(me_b + k, nb))

    barrier = pltpu.get_barrier_semaphore()

    def greet(peer):
        pl.semaphore_signal(barrier, inc=1, device_id=peer, device_id_type=MESH)

    each(nd, lambda k: greet(crop_peer(k)))
    each(nb, lambda k: greet(band_peer(k)))

    row_i = lax.broadcasted_iota(jnp.int32, (rows_all, lanes), 0)
    lane_i = lax.broadcasted_iota(jnp.int32, (rows_all, lanes), 1)
    block = lane_i // rows_all
    tap = lane_i % rows_all - row_i + half
    band_mask[...] = jnp.where((tap >= 0) & (tap < ks) & (block < ks), 1.0, 0.0)
    col = lax.broadcasted_iota(jnp.int32, (rows_all, width), 1)
    for j in range(ks):
        inside = (col + (j - half) >= 0) & (col + (j - half) < width)
        edge[j] = jnp.where(inside, 1.0, 0.0).astype(BF16)
    for h in range(rows_all):
        filt[pl.ds(h * fs + bp - 16, 16), :] = jnp.zeros((16, width), F32)

    place_j = lax.broadcasted_iota(jnp.int32, (ks, lanes), 0)
    place_l = lax.broadcasted_iota(jnp.int32, (ks, lanes), 1) - (8 - half)
    base = jnp.zeros((bands, lanes), F32)
    for i in range(ks):
        spot = jnp.where(place_l == place_j * rows_all + i, 1.0, 0.0).astype(BF16)
        base = base + mm_tn(taps_ref[i], spot)
    tap_rows[0:bands, :] = base

    def over_bands(lo, hi, act):
        def body(g, _):
            stores = [act(g * unroll + q) for q in range(unroll)]
            for store in stores:
                store()
            return 0

        lax.fori_loop(lo, hi, body, 0)

    half_rows = rows if split else rows_all

    def shift_band(b):
        image = x_ref[b]
        parts = []
        for j in range(ks):
            s = j - half
            parts.append(image if s == 0 else pltpu.roll(image, (-s) % width, 1) * edge[j])
        parts.append(jnp.zeros((lanes - ks * rows_all, width), BF16))
        spread = jnp.broadcast_to(tap_rows[pl.ds(b, 1), :], (rows_all, lanes))
        taps = pltpu.roll(spread, lanes - 8, 1, stride=1, stride_axis=0)
        taps = (taps * band_mask[...]).astype(BF16)

        def store():
            for j in range(len(parts)):
                size = parts[j].shape[0]
                stack[b, j * rows_all:j * rows_all + size, :] = parts[j]
            for k in range(rows_all // half_rows):
                taps_all[k, b] = taps[k * half_rows:(k + 1) * half_rows]

        return store

    def filter_part(part):
        first = part * half_rows * fs

        def filter_band(b):
            out = mm(taps_all[part, b], stack[b]).astype(BF16).astype(F32)

            def store():
                filt[pl.ds(first + b, half_rows, stride=fs), :] = out

            return store

        over_bands(0, groups, filter_band)

    groups = bands // unroll
    over_bands(0, groups, shift_band)
    filter_part(1 - me_b if split else 0)

    pick = jnp.where(
        lax.broadcasted_iota(jnp.int32, (bp, outs), 1)
        == lax.broadcasted_iota(jnp.int32, (bp, outs), 0) + me_b * bands,
        1.0, 0.0,
    )
    pick = jnp.where(lax.broadcasted_iota(jnp.int32, (bp, outs), 0) < bands, pick, 0.0).astype(BF16)
    wft_ref[...] = mm_nt(w1t_ref[...], pick).astype(BF16)

    def filt_rows(h, count):
        return jnp.concatenate(
            [
                filt[pl.ds(pl.multiple_of((h + r) * fs, 8), bp), :].astype(BF16)
                for r in range(count)
            ],
            axis=1,
        )

    pl.semaphore_wait(barrier, nd + nb - 2)

    def z_copy(k, c):
        part = pl.ds(c * step_rows, step_rows)
        return pltpu.make_async_remote_copy(
            src_ref=z_send.at[k, part],
            dst_ref=z_recv.at[k, part],
            send_sem=z_ss.at[k, c],
            recv_sem=z_rs.at[k, c],
            device_id=(me_d, lax.rem(me_b + k, nb)),
            device_id_type=MESH,
        )

    def z_part(k, c):
        owner = lax.rem(me_b + k, nb)

        def one(p, _):
            h = c * step_rows + p * 2
            z = mm(wft_ref[...], filt_rows(owner * rows + h, 2))
            z_send[k, h] = z[:, :width]
            z_send[k, h + 1] = z[:, width:]
            return 0

        lax.fori_loop(0, step_rows // 2, one, 0, unroll=True)

    for k in range(1, nb):
        for c in range(chunks):
            z_part(k, c)
            z_copy(k, c).start()
    if split:
        filter_part(me_b)
    for c in range(chunks):
        z_part(0, c)
    wf_ref[...] = mm_nt(pick, w1t_ref[...]).astype(BF16)
    wmt_ref[...] = mm_nt(eye(ch), wm_ref[...]).astype(BF16)
    wot_ref[...] = mm_nt(eye(outs), wo_ref[...]).astype(BF16)
    if ts == rows:
        wanted[...] = target_ref[...].astype(F32)
    else:
        def widen(g, _):
            for q in range(8):
                o = g * 8 + q
                block_o = target_ref[pl.ds(pl.multiple_of(o * rows, 16), rows), :]
                wanted[pl.ds(pl.multiple_of(o * ts, 8), rows), :] = block_o.astype(F32)
            return 0

        lax.fori_loop(0, outs // 8, widen, 0)

    def d_copy(k, c):
        part = pl.ds(me_b * rows + c * step_rows, step_rows)
        return pltpu.make_async_remote_copy(
            src_ref=dz_all.at[part],
            dst_ref=dz_all.at[part],
            send_sem=d_ss.at[k, c],
            recv_sem=d_rs.at[k, c],
            device_id=(me_d, lax.rem(me_b + k, nb)),
            device_id_type=MESH,
        )

    def wide(pieces):
        return jnp.concatenate(pieces, axis=1)

    g_out = jnp.zeros((ch, outs), F32)
    g_mid = jnp.zeros((ch, ch), F32)
    for c in range(chunks):
        for k in range(1, nb):
            z_copy(k, c).wait_recv()
        z_list = []
        for r in range(step_rows):
            h = c * step_rows + r
            z = z_send[0, h]
            for k in range(1, nb):
                z = z + z_recv[k, h]
            z_list.append(z)
        z_first = wide(z_list)
        sig_first = jax.nn.sigmoid(z_first)
        hid_first = (z_first * sig_first).astype(BF16)
        z_mid = mm(wmt_ref[...], hid_first)
        sig_mid = jax.nn.sigmoid(z_mid)
        hid_mid = (hid_first.astype(F32) + z_mid * sig_mid).astype(BF16)
        predicted = mm(wot_ref[...], hid_mid)
        errs = []
        for r in range(step_rows):
            h = c * step_rows + r
            factor = (2.0 * scale) * mask_ref[pl.ds(h, 1), :].astype(F32)
            diff = predicted[:, r * width:(r + 1) * width] - wanted[pl.ds(h, outs, stride=ts), :]
            errs.append((factor * diff).astype(BF16))
        err = wide(errs)
        g_out = g_out + mm_nt(hid_mid, err)
        d_mid = mm(wo_ref[...], err)
        dz_mid = (d_mid * (sig_mid * (1.0 + z_mid * (1.0 - sig_mid)))).astype(BF16)
        g_mid = g_mid + mm_nt(hid_first, dz_mid)
        d_first = d_mid + mm(wm_ref[...], dz_mid)
        dz = (d_first * (sig_first * (1.0 + z_first * (1.0 - sig_first)))).astype(BF16)
        for r in range(step_rows):
            h = c * step_rows + r
            dz_all[me_b * rows + h] = dz[:, r * width:(r + 1) * width]
        for k in range(1, nb):
            d_copy(k, c).start()

    def piece(ref, index, w):
        lane_parts = nd // 8
        each_w = w // lane_parts
        return ref.at[
            pl.ds(pl.multiple_of((index // lane_parts) * 8, 8), 8),
            pl.ds(pl.multiple_of(lax.rem(index, lane_parts) * each_w, 128), each_w),
        ]

    def remote(src, dst, ss, rs, peer):
        return pltpu.make_async_remote_copy(
            src_ref=src, dst_ref=dst, send_sem=ss, recv_sem=rs,
            device_id=peer, device_id_type=MESH,
        )

    def scatter(ref, into, w, ss, rs):
        def start(k):
            peer = crop_peer(k)
            remote(piece(ref, peer[0], w), into.at[k], ss, rs, peer).start()

        each(nd, start)

    def gather(out, ss, rs):
        def start(k):
            remote(out.at[me_d], out.at[me_d], ss, rs, crop_peer(k)).start()

        each(nd, start)

    def wait_all(ref, sem):
        rest = ref.at[pl.ds(1, nd - 1)]
        pltpu.make_async_copy(rest, rest, sem).wait()

    def add_up(ref, into, w):
        own = piece(ref, me_d, w)[...]
        for k in range(1, nd):
            own = own + into[k]
        return own

    def band_early(k):
        return remote(
            early_out.at[me_d, me_b], early_out.at[me_d, me_b], ex_ss.at[k], ex_rs.at[k], band_peer(k)
        )

    def spread_out(out, w, put):
        lane_parts = nd // 8
        each_w = w // lane_parts
        for d in range(nd):
            put(out, d, (d // lane_parts) * 8, (d % lane_parts) * each_w, each_w)

    early[...] = jnp.zeros_like(early)
    late[...] = jnp.zeros_like(late)
    sums[...] = jnp.zeros_like(sums)

    hid_s[...] = jnp.zeros_like(hid_s)

    def slope_rows(first):
        def one(p, _):
            h = first + 2 * p
            dz = wide([dz_all[h], dz_all[h + 1]])
            hid_s[...] += mm_nt(dz, filt_rows(h, 2))
            back = mm(wf_ref[...], dz)
            for r in range(2):
                place = pl.multiple_of((rows_all - 1 - h - r) * fs, 8)
                slope[pl.ds(place, bp), :] = back[:, r * width:(r + 1) * width]
            return 0

        lax.fori_loop(0, step_rows // 2, one, 0, unroll=True)

    skew = lanes - (rows_all - 1) + half
    extra = -skew % 8

    lane = lax.rem(lane_i + (lanes - extra), lanes)
    tap_e = lane % rows_all
    source_e = rows_all - 1 - row_i + tap_e - half
    valid = (lane < ks * rows_all) & (tap_e < ks) & (source_e >= 0) & (source_e < rows_all)
    diag_mask[...] = jnp.where(valid, 1.0, 0.0)

    def taps_band(b):
        rows_b = slope[pl.ds(b, rows_all, stride=fs), :].astype(BF16)
        cross = mm_nt(rows_b, stack[b])
        moved = pltpu.roll(cross, (skew + extra) % lanes, 1, stride=1, stride_axis=0)
        moved = moved * diag_mask[...]
        acc = moved[0:8]
        for r in range(8, rows_all, 8):
            acc = acc + moved[r:r + 8]

        def store():
            place = pl.ds(pl.multiple_of(b * 8, 8), 8)
            for part in range(lanes // 128):
                sums[part, place, :] = acc[:, part * 128:(part + 1) * 128]

        return store

    for c in range(chunks):
        slope_rows(me_b * rows + c * step_rows)
    for k in range(1, nb):
        source = lax.rem(me_b + nb - k, nb)
        for c in range(chunks):
            d_copy(k, c).wait_recv()
            slope_rows(source * rows + c * step_rows)

    early[:, 0:outs] = g_out
    early[:, outs:outs + ch] = g_mid
    early[:, outs + ch:outs + ch + bands] = hid_s[:, 0:bands]
    scatter(early, early_in, ew, e_ss, e_rs)

    first, second = groups * 2 // 5, groups * 7 // 10
    over_bands(0, first, taps_band)

    wait_all(early_in, e_rs)
    early_out[me_d, me_b] = add_up(early, early_in, ew)
    for k in range(1, nb):
        band_early(k).start()

    over_bands(first, second, taps_band)

    for k in range(1, nb):
        band_early(k).wait_recv()
    gather(early_out, ea_ss, ea_rs)

    over_bands(second, groups, taps_band)

    slot_r = lax.broadcasted_iota(jnp.int32, (8 * ks, lanes), 0)
    slot_l = lax.broadcasted_iota(jnp.int32, (8 * ks, lanes), 1) - extra
    spot = jnp.where(slot_l == (slot_r % 8) * rows_all + slot_r // 8, 1.0, 0.0)
    parts = []
    for part in range(lanes // 128):
        rows_sum = sums[part, pl.ds(0, bp, stride=8), :]
        for r in range(1, 8):
            rows_sum = rows_sum + sums[part, pl.ds(r, bp, stride=8), :]
        parts.append(rows_sum)
    per_band = wide(parts)
    late[0:8 * ks, 0:bp] = lax.dot_general(
        spot, per_band, (((1,), (1,)), ((), ())),
        preferred_element_type=F32, precision=lax.Precision.HIGHEST,
    )
    scatter(late, late_in, lw, l_ss, l_rs)

    wait_all(early_out, ea_rs)

    def put_early(out, d, r, w0, w):
        both = out[d, 0]
        for k in range(1, nb):
            both = both + out[d, k]
        total_ref[r:r + 8, w0:w0 + w] = both
        for k in range(nb):
            sides[k, r:r + 8, w0:w0 + w] = out[d, k]

    spread_out(early_out, ew, put_early)
    go_ref[...] = total_ref[:, 0:outs]
    gm_ref[...] = total_ref[:, outs:outs + ch]
    for k in range(nb):
        gf_ref[:, k * bands:(k + 1) * bands] = sides[k, :, outs + ch:outs + ch + bands]

    wait_all(late_in, l_rs)
    late_out[me_d] = add_up(late, late_in, lw)
    gather(late_out, la_ss, la_rs)
    for k in range(1, nb):
        band_early(k).wait_send()
        for c in range(chunks):
            z_copy(k, c).wait_send()
            d_copy(k, c).wait_send()
    wait_all(early_in, e_ss)
    wait_all(early_out, ea_ss)
    wait_all(late_in, l_ss)
    wait_all(late_out, la_rs)

    def put_late(out, d, r, w0, w):
        gk_ref[r:r + 8, w0:w0 + w] = out[d]

    spread_out(late_out, lw, put_late)
    wait_all(late_out, la_ss)


def finish(gk_in, gf_in, gm_in, go_in, gk_out, gf_out, gm_out, go_out):
    ks, _, bands = gk_out.shape
    for i in range(ks):
        gk_out[i] = gk_in[8 * i:8 * i + ks, 0:bands]
    gf_out[...] = gf_in[...]
    gm_out[...] = gm_in[...]
    go_out[...] = go_in[...]


def on_device(nd, nb, radiance, kernel_taps, w_first, w_mid, w_out, target, mask):
    image = radiance[0]
    bands, rows_all, width = image.shape
    ks = kernel_taps.shape[1]
    ch = w_first.shape[1]
    outs = w_out.shape[1]
    rows = rows_all // nb
    chunks = min(4, rows // 2)
    unroll = max(u for u in range(1, 11) if bands % u == 0)
    bp = up(bands, 16)
    fs = bp + 8
    ts = rows + 8 if rows % 16 == 0 and outs % 8 == 0 else rows
    lane_parts = nd // 8
    lanes = 8 * rows_all
    ew = up(outs + ch + bands, 128 * lane_parts)
    lw = up(bp, 128 * lane_parts)
    cfg = dict(
        nd=nd, nb=nb, bands=bands, unroll=unroll, bp=bp, ks=ks, rows_all=rows_all, rows=rows,
        width=width, chunks=chunks, ch=ch, outs=outs, ew=ew, lw=lw, fs=fs, ts=ts,
        scale=1.0 / math.sqrt(nd * rows_all * width),
    )
    sems = lambda *shape: pltpu.SemaphoreType.DMA(shape)
    vmem = pl.BlockSpec(memory_space=pltpu.VMEM)
    sums = pl.pallas_call(
        functools.partial(kernel, cfg),
        out_shape=(
            jax.ShapeDtypeStruct((64, lw), F32),
            jax.ShapeDtypeStruct((ch, bands * nb), F32),
            jax.ShapeDtypeStruct((ch, ch), F32),
            jax.ShapeDtypeStruct((ch, outs), F32),
        ),
        in_specs=[vmem] * 7,
        out_specs=(vmem,) * 4,
        scratch_shapes=[
            pltpu.VMEM((rows_all, lanes), F32),
            pltpu.VMEM((ks, rows_all, width), BF16),
            pltpu.VMEM((rows_all, lanes), F32),
            pltpu.VMEM((bp, lanes), F32),
            pltpu.VMEM((2, bands, rows_all // 2, lanes) if nb == 2 else (1, bands, rows_all, lanes), BF16),
            pltpu.VMEM((ch, bp), BF16),
            pltpu.VMEM((bp, ch), BF16),
            pltpu.VMEM((ch, ch), BF16),
            pltpu.VMEM((outs, ch), BF16),
            pltpu.VMEM((outs * ts, width), F32),
            pltpu.VMEM((lanes // 128, 8 * bp, 128), F32),
            pltpu.VMEM((bands, lanes, width), BF16),
            pltpu.VMEM((rows_all * fs, width), F32),
            pltpu.VMEM((rows_all * fs, width), F32),
            pltpu.VMEM((nb, rows, ch, width), F32),
            pltpu.VMEM((nb, rows, ch, width), F32),
            pltpu.VMEM((rows_all, ch, width), BF16),
            pltpu.VMEM((ch, bp), F32),
            pltpu.VMEM((64, ew), F32),
            pltpu.VMEM((nd, 8, ew // lane_parts), F32),
            pltpu.VMEM((nd, nb, 8, ew // lane_parts), F32),
            pltpu.VMEM((64, ew), F32),
            pltpu.VMEM((nb, 64, ew), F32),
            pltpu.VMEM((64, lw), F32),
            pltpu.VMEM((nd, 8, lw // lane_parts), F32),
            pltpu.VMEM((nd, 8, lw // lane_parts), F32),
            sems(nb, chunks), sems(nb, chunks), sems(nb, chunks), sems(nb, chunks),
            sems(nb), sems(nb), *[pltpu.SemaphoreType.DMA] * 8,
        ],
        compiler_params=pltpu.CompilerParams(
            collective_id=0, has_side_effects=True, vmem_limit_bytes=56 * 1024 * 1024
        ),
    )(
        image, kernel_taps.transpose(1, 2, 0), w_first.T, w_mid, w_out,
        target[0].reshape(outs * rows, width), mask[0],
    )
    g_taps, g_first, g_mid, g_out = pl.pallas_call(
        finish,
        out_shape=(
            jax.ShapeDtypeStruct((ks, ks, bands), F32),
            jax.ShapeDtypeStruct((ch, bands * nb), F32),
            jax.ShapeDtypeStruct((ch, ch), F32),
            jax.ShapeDtypeStruct((ch, outs), F32),
        ),
        in_specs=[vmem] * 4,
        out_specs=(vmem,) * 4,
    )(*sums)
    return (g_taps.transpose(2, 0, 1), g_first.T, g_mid, g_out)


def solution(mesh):
    in_specs = (
        P("dp", "band", None, None),
        P("band", None, None),
        P(),
        P(),
        P(),
        P("dp", None, "band", None),
        P("dp", "band", None),
    )
    out_specs = (P("band", None, None), P(), P(), P())
    return jax.shard_map(
        functools.partial(on_device, mesh.shape["dp"], mesh.shape["band"]),
        mesh=mesh, in_specs=in_specs, out_specs=out_specs, check_vma=False,
    )
```

```python
import functools
import math

import jax
import jax.numpy as jnp
from jax import lax
from jax.experimental import pallas as pl
from jax.experimental.pallas import tpu as pltpu
from jax.sharding import PartitionSpec as P

MESH = pl.DeviceIdType.MESH
F32 = jnp.float32
BF16 = jnp.bfloat16


def up(value, step):
    return -(-value // step) * step


def mm(a, b):
    return jnp.dot(a, b, preferred_element_type=F32)


def mm_tn(a, b):
    return lax.dot_general(a, b, (((0,), (0,)), ((), ())), preferred_element_type=F32)


def eye(n):
    same = lax.broadcasted_iota(jnp.int32, (n, n), 0) == lax.broadcasted_iota(jnp.int32, (n, n), 1)
    return jnp.where(same, 1.0, 0.0).astype(BF16)


def mm_nt(a, b):
    return lax.dot_general(a, b, (((1,), (1,)), ((), ())), preferred_element_type=F32)


def kernel(
    cfg,
    x_ref, taps_ref, w1t_ref, wm_ref, wo_ref, target_ref, mask_ref,
    gk_ref, gf_ref, gm_ref, go_ref,
    band_mask, edge, diag_mask, tap_rows, taps_own, wft_ref, wf_ref, wmt_ref, wot_ref, wanted, sums, stack, filt, slope, z_send, z_recv, dz_all, hid_s,
    early, early_in, early_out, total_ref, sides, late, late_in, late_out,
    z_ss, z_rs, d_ss, d_rs, ex_ss, ex_rs, e_ss, e_rs, ea_ss, ea_rs, l_ss, l_rs, la_ss, la_rs,
):
    nd, nb = cfg["nd"], cfg["nb"]
    bands, unroll, bp, ks = cfg["bands"], cfg["unroll"], cfg["bp"], cfg["ks"]
    fs, ts = cfg["fs"], cfg["ts"]
    rows_all, rows, width, chunks = cfg["rows_all"], cfg["rows"], cfg["width"], cfg["chunks"]
    ch, outs, scale = cfg["ch"], cfg["outs"], cfg["scale"]
    ew, lw = cfg["ew"], cfg["lw"]
    half = ks // 2
    lanes = 8 * rows_all
    step_rows = rows // chunks
    me_d = lax.axis_index("dp")
    me_b = lax.axis_index("band")
    split = nb == 2

    def each(count, act):
        if count <= 16:
            for k in range(1, count):
                act(k)
            return

        def body(k, _):
            act(k)
            return 0

        lax.fori_loop(1, count, body, 0)

    def crop_peer(k):
        return (lax.rem(me_d + k, nd), me_b)

    def band_peer(k):
        return (me_d, lax.rem(me_b + k, nb))

    barrier = pltpu.get_barrier_semaphore()

    def greet(peer):
        pl.semaphore_signal(barrier, inc=1, device_id=peer, device_id_type=MESH)

    each(nd, lambda k: greet(crop_peer(k)))
    each(nb, lambda k: greet(band_peer(k)))

    row_i = lax.broadcasted_iota(jnp.int32, (rows_all, lanes), 0)
    lane_i = lax.broadcasted_iota(jnp.int32, (rows_all, lanes), 1)
    block = lane_i // rows_all
    tap = lane_i % rows_all - row_i + half
    band_mask[...] = jnp.where((tap >= 0) & (tap < ks) & (block < ks), 1.0, 0.0)
    col = lax.broadcasted_iota(jnp.int32, (rows_all, width), 1)
    for j in range(ks):
        inside = (col + (j - half) >= 0) & (col + (j - half) < width)
        edge[j] = jnp.where(inside, 1.0, 0.0).astype(BF16)
    for h in range(rows_all):
        filt[pl.ds(h * fs + bp - 16, 16), :] = jnp.zeros((16, width), F32)

    place_j = lax.broadcasted_iota(jnp.int32, (ks, lanes), 0)
    place_l = lax.broadcasted_iota(jnp.int32, (ks, lanes), 1) - (8 - half)
    base = jnp.zeros((bands, lanes), F32)
    for i in range(ks):
        spot = jnp.where(place_l == place_j * rows_all + i, 1.0, 0.0).astype(BF16)
        base = base + mm_tn(taps_ref[i], spot)
    tap_rows[0:bands, :] = base

    lower = me_b == 0
    mid_row = rows_all // 2

    def filter_band(b):
        image = x_ref[b]
        parts = []
        for j in range(ks):
            s = j - half
            if s == 0:
                moved = image
            else:
                moved = pltpu.roll(image, (-s) % width, 1) * edge[j]
            parts.append(moved)
        parts.append(jnp.zeros((lanes - ks * rows_all, width), BF16))
        moved_all = jnp.concatenate(parts, axis=0)
        stack[b] = moved_all
        spread = jnp.broadcast_to(tap_rows[pl.ds(b, 1), :], (rows_all, lanes))
        taps = pltpu.roll(spread, lanes - 8, 1, stride=1, stride_axis=0)
        taps = taps * band_mask[...]
        if split:
            taps_own[b] = jnp.where(lower, taps[:mid_row], taps[mid_row:]).astype(BF16)
            taps = jnp.where(lower, taps[mid_row:], taps[:mid_row])
            first, count = (1 - me_b) * rows, rows
        else:
            first, count = 0, rows_all
        out = mm(taps.astype(BF16), moved_all)
        filt[pl.ds(first * fs + b, count, stride=fs), :] = out.astype(BF16).astype(F32)

    def filter_own(b):
        out = mm(taps_own[b], stack[b])
        filt[pl.ds(me_b * rows * fs + b, rows, stride=fs), :] = out.astype(BF16).astype(F32)

    def over_bands(lo, hi, act):
        def body(g, _):
            for q in range(unroll):
                act(g * unroll + q)
            return 0

        lax.fori_loop(lo, hi, body, 0)

    groups = bands // unroll
    over_bands(0, groups, filter_band)

    pick = jnp.where(
        lax.broadcasted_iota(jnp.int32, (bp, outs), 1)
        == lax.broadcasted_iota(jnp.int32, (bp, outs), 0) + me_b * bands,
        1.0, 0.0,
    )
    pick = jnp.where(lax.broadcasted_iota(jnp.int32, (bp, outs), 0) < bands, pick, 0.0).astype(BF16)
    wft_ref[...] = mm_nt(w1t_ref[...], pick).astype(BF16)

    def filt_rows(h, count):
        return jnp.concatenate(
            [
                filt[pl.ds(pl.multiple_of((h + r) * fs, 8), bp), :].astype(BF16)
                for r in range(count)
            ],
            axis=1,
        )

    pl.semaphore_wait(barrier, nd + nb - 2)

    def z_copy(k, c):
        part = pl.ds(c * step_rows, step_rows)
        return pltpu.make_async_remote_copy(
            src_ref=z_send.at[k, part],
            dst_ref=z_recv.at[k, part],
            send_sem=z_ss.at[k, c],
            recv_sem=z_rs.at[k, c],
            device_id=(me_d, lax.rem(me_b + k, nb)),
            device_id_type=MESH,
        )

    def z_part(k, c):
        owner = lax.rem(me_b + k, nb)

        def one(p, _):
            h = c * step_rows + p * 2
            z = mm(wft_ref[...], filt_rows(owner * rows + h, 2))
            z_send[k, h] = z[:, :width]
            z_send[k, h + 1] = z[:, width:]
            return 0

        lax.fori_loop(0, step_rows // 2, one, 0, unroll=True)

    for k in range(1, nb):
        for c in range(chunks):
            z_part(k, c)
            z_copy(k, c).start()
    if split:
        over_bands(0, groups, filter_own)
    for c in range(chunks):
        z_part(0, c)
    wf_ref[...] = mm_nt(pick, w1t_ref[...]).astype(BF16)
    wmt_ref[...] = mm_nt(eye(ch), wm_ref[...]).astype(BF16)
    wot_ref[...] = mm_nt(eye(outs), wo_ref[...]).astype(BF16)
    if ts == rows:
        wanted[...] = target_ref[...].astype(F32)
    else:
        def widen(g, _):
            for q in range(8):
                o = g * 8 + q
                block_o = target_ref[pl.ds(pl.multiple_of(o * rows, 16), rows), :]
                wanted[pl.ds(pl.multiple_of(o * ts, 8), rows), :] = block_o.astype(F32)
            return 0

        lax.fori_loop(0, outs // 8, widen, 0)

    early[...] = jnp.zeros_like(early)
    late[...] = jnp.zeros_like(late)
    sums[...] = jnp.zeros_like(sums)

    skew = lanes - (rows_all - 1) + half
    extra = -skew % 8

    lane = lax.rem(lane_i + (lanes - extra), lanes)
    tap_e = lane % rows_all
    source_e = rows_all - 1 - row_i + tap_e - half
    valid = (lane < ks * rows_all) & (tap_e < ks) & (source_e >= 0) & (source_e < rows_all)
    diag_mask[...] = jnp.where(valid, 1.0, 0.0)

    def d_copy(k, c):
        part = pl.ds(me_b * rows + c * step_rows, step_rows)
        return pltpu.make_async_remote_copy(
            src_ref=dz_all.at[part],
            dst_ref=dz_all.at[part],
            send_sem=d_ss.at[k, c],
            recv_sem=d_rs.at[k, c],
            device_id=(me_d, lax.rem(me_b + k, nb)),
            device_id_type=MESH,
        )

    def wide(pieces):
        return jnp.concatenate(pieces, axis=1)

    hid_s[...] = jnp.zeros_like(hid_s)

    def slope_rows(first):
        def one(p, _):
            h = first + 2 * p
            dz = wide([dz_all[h], dz_all[h + 1]])
            hid_s[...] += mm_nt(dz, filt_rows(h, 2))
            back = mm(wf_ref[...], dz)
            for r in range(2):
                place = pl.multiple_of((rows_all - 1 - h - r) * fs, 8)
                slope[pl.ds(place, bp), :] = back[:, r * width:(r + 1) * width]
            return 0

        lax.fori_loop(0, step_rows // 2, one, 0, unroll=True)

    def others_slopes(c):
        for k in range(1, nb):
            d_copy(k, c).wait_recv()
            slope_rows(lax.rem(me_b + nb - k, nb) * rows + c * step_rows)

    g_out = jnp.zeros((ch, outs), F32)
    g_mid = jnp.zeros((ch, ch), F32)
    for c in range(chunks):
        for k in range(1, nb):
            z_copy(k, c).wait_recv()
        z_list = []
        for r in range(step_rows):
            h = c * step_rows + r
            z = z_send[0, h]
            for k in range(1, nb):
                z = z + z_recv[k, h]
            z_list.append(z)
        z_first = wide(z_list)
        sig_first = jax.nn.sigmoid(z_first)
        hid_first = (z_first * sig_first).astype(BF16)
        z_mid = mm(wmt_ref[...], hid_first)
        sig_mid = jax.nn.sigmoid(z_mid)
        hid_mid = (hid_first.astype(F32) + z_mid * sig_mid).astype(BF16)
        predicted = mm(wot_ref[...], hid_mid)
        errs = []
        for r in range(step_rows):
            h = c * step_rows + r
            factor = (2.0 * scale) * mask_ref[pl.ds(h, 1), :].astype(F32)
            diff = predicted[:, r * width:(r + 1) * width] - wanted[pl.ds(h, outs, stride=ts), :]
            errs.append((factor * diff).astype(BF16))
        err = wide(errs)
        g_out = g_out + mm_nt(hid_mid, err)
        d_mid = mm(wo_ref[...], err)
        dz_mid = (d_mid * (sig_mid * (1.0 + z_mid * (1.0 - sig_mid)))).astype(BF16)
        g_mid = g_mid + mm_nt(hid_first, dz_mid)
        d_first = d_mid + mm(wm_ref[...], dz_mid)
        dz = (d_first * (sig_first * (1.0 + z_first * (1.0 - sig_first)))).astype(BF16)
        for r in range(step_rows):
            h = c * step_rows + r
            dz_all[me_b * rows + h] = dz[:, r * width:(r + 1) * width]
        for k in range(1, nb):
            d_copy(k, c).start()
        slope_rows(me_b * rows + c * step_rows)
        if c > 0:
            others_slopes(c - 1)
    others_slopes(chunks - 1)

    def piece(ref, index, w):
        lane_parts = nd // 8
        each_w = w // lane_parts
        return ref.at[
            pl.ds(pl.multiple_of((index // lane_parts) * 8, 8), 8),
            pl.ds(pl.multiple_of(lax.rem(index, lane_parts) * each_w, 128), each_w),
        ]

    def remote(src, dst, ss, rs, peer):
        return pltpu.make_async_remote_copy(
            src_ref=src, dst_ref=dst, send_sem=ss, recv_sem=rs,
            device_id=peer, device_id_type=MESH,
        )

    def scatter(ref, into, w, ss, rs):
        def start(k):
            peer = crop_peer(k)
            remote(piece(ref, peer[0], w), into.at[k], ss, rs, peer).start()

        each(nd, start)

    def gather(out, ss, rs):
        def start(k):
            remote(out.at[me_d], out.at[me_d], ss, rs, crop_peer(k)).start()

        each(nd, start)

    def wait_all(ref, sem):
        rest = ref.at[pl.ds(1, nd - 1)]
        pltpu.make_async_copy(rest, rest, sem).wait()

    def add_up(ref, into, w):
        own = piece(ref, me_d, w)[...]
        for k in range(1, nd):
            own = own + into[k]
        return own

    def band_early(k):
        return remote(
            early_out.at[me_d, me_b], early_out.at[me_d, me_b], ex_ss.at[k], ex_rs.at[k], band_peer(k)
        )

    def spread_out(out, w, put):
        lane_parts = nd // 8
        each_w = w // lane_parts
        for d in range(nd):
            put(out, d, (d // lane_parts) * 8, (d % lane_parts) * each_w, each_w)

    def taps_band(b):
        rows_b = slope[pl.ds(b, rows_all, stride=fs), :].astype(BF16)
        cross = mm_nt(rows_b, stack[b])
        moved = pltpu.roll(cross, (skew + extra) % lanes, 1, stride=1, stride_axis=0)
        moved = moved * diag_mask[...]
        acc = moved[0:8]
        for r in range(8, rows_all, 8):
            acc = acc + moved[r:r + 8]
        for part in range(lanes // 128):
            sums[part, pl.ds(pl.multiple_of(b * 8, 8), 8), :] = acc[:, part * 128:(part + 1) * 128]

    early[:, 0:outs] = g_out
    early[:, outs:outs + ch] = g_mid
    early[:, outs + ch:outs + ch + bands] = hid_s[:, 0:bands]
    scatter(early, early_in, ew, e_ss, e_rs)

    first, second = groups * 2 // 5, groups * 7 // 10
    over_bands(0, first, taps_band)

    wait_all(early_in, e_rs)
    early_out[me_d, me_b] = add_up(early, early_in, ew)
    for k in range(1, nb):
        band_early(k).start()

    over_bands(first, second, taps_band)

    for k in range(1, nb):
        band_early(k).wait_recv()
    gather(early_out, ea_ss, ea_rs)

    over_bands(second, groups, taps_band)

    slot_r = lax.broadcasted_iota(jnp.int32, (8 * ks, lanes), 0)
    slot_l = lax.broadcasted_iota(jnp.int32, (8 * ks, lanes), 1) - extra
    spot = jnp.where(slot_l == (slot_r % 8) * rows_all + slot_r // 8, 1.0, 0.0)
    parts = []
    for part in range(lanes // 128):
        rows_sum = sums[part, pl.ds(0, bp, stride=8), :]
        for r in range(1, 8):
            rows_sum = rows_sum + sums[part, pl.ds(r, bp, stride=8), :]
        parts.append(rows_sum)
    per_band = wide(parts)
    late[0:8 * ks, 0:bp] = lax.dot_general(
        spot, per_band, (((1,), (1,)), ((), ())),
        preferred_element_type=F32, precision=lax.Precision.HIGHEST,
    )
    scatter(late, late_in, lw, l_ss, l_rs)

    wait_all(early_out, ea_rs)

    def put_early(out, d, r, w0, w):
        both = out[d, 0]
        for k in range(1, nb):
            both = both + out[d, k]
        total_ref[r:r + 8, w0:w0 + w] = both
        for k in range(nb):
            sides[k, r:r + 8, w0:w0 + w] = out[d, k]

    spread_out(early_out, ew, put_early)
    go_ref[...] = total_ref[:, 0:outs]
    gm_ref[...] = total_ref[:, outs:outs + ch]
    for k in range(nb):
        gf_ref[:, k * bands:(k + 1) * bands] = sides[k, :, outs + ch:outs + ch + bands]

    wait_all(late_in, l_rs)
    late_out[me_d] = add_up(late, late_in, lw)
    gather(late_out, la_ss, la_rs)
    for k in range(1, nb):
        band_early(k).wait_send()
        for c in range(chunks):
            z_copy(k, c).wait_send()
            d_copy(k, c).wait_send()
    wait_all(early_in, e_ss)
    wait_all(early_out, ea_ss)
    wait_all(late_in, l_ss)
    wait_all(late_out, la_rs)

    def put_late(out, d, r, w0, w):
        gk_ref[r:r + 8, w0:w0 + w] = out[d]

    spread_out(late_out, lw, put_late)
    wait_all(late_out, la_ss)


def finish(gk_in, gf_in, gm_in, go_in, gk_out, gf_out, gm_out, go_out):
    ks, _, bands = gk_out.shape
    for i in range(ks):
        gk_out[i] = gk_in[8 * i:8 * i + ks, 0:bands]
    gf_out[...] = gf_in[...]
    gm_out[...] = gm_in[...]
    go_out[...] = go_in[...]


def on_device(nd, nb, radiance, kernel_taps, w_first, w_mid, w_out, target, mask):
    image = radiance[0]
    bands, rows_all, width = image.shape
    ks = kernel_taps.shape[1]
    ch = w_first.shape[1]
    outs = w_out.shape[1]
    rows = rows_all // nb
    chunks = min(8, rows // 2)
    unroll = max(u for u in range(1, 11) if bands % u == 0)
    bp = up(bands, 16)
    fs = bp + 8
    ts = rows + 8 if rows % 16 == 0 and outs % 8 == 0 else rows
    lane_parts = nd // 8
    lanes = 8 * rows_all
    ew = up(outs + ch + bands, 128 * lane_parts)
    lw = up(bp, 128 * lane_parts)
    cfg = dict(
        nd=nd, nb=nb, bands=bands, unroll=unroll, bp=bp, ks=ks, rows_all=rows_all, rows=rows,
        width=width, chunks=chunks, ch=ch, outs=outs, ew=ew, lw=lw, fs=fs, ts=ts,
        scale=1.0 / math.sqrt(nd * rows_all * width),
    )
    sems = lambda *shape: pltpu.SemaphoreType.DMA(shape)
    vmem = pl.BlockSpec(memory_space=pltpu.VMEM)
    sums = pl.pallas_call(
        functools.partial(kernel, cfg),
        out_shape=(
            jax.ShapeDtypeStruct((64, lw), F32),
            jax.ShapeDtypeStruct((ch, bands * nb), F32),
            jax.ShapeDtypeStruct((ch, ch), F32),
            jax.ShapeDtypeStruct((ch, outs), F32),
        ),
        in_specs=[vmem] * 7,
        out_specs=(vmem,) * 4,
        scratch_shapes=[
            pltpu.VMEM((rows_all, lanes), F32),
            pltpu.VMEM((ks, rows_all, width), BF16),
            pltpu.VMEM((rows_all, lanes), F32),
            pltpu.VMEM((bp, lanes), F32),
            pltpu.VMEM((bands, rows_all // 2, lanes), BF16),
            pltpu.VMEM((ch, bp), BF16),
            pltpu.VMEM((bp, ch), BF16),
            pltpu.VMEM((ch, ch), BF16),
            pltpu.VMEM((outs, ch), BF16),
            pltpu.VMEM((outs * ts, width), F32),
            pltpu.VMEM((lanes // 128, 8 * bp, 128), F32),
            pltpu.VMEM((bands, lanes, width), BF16),
            pltpu.VMEM((rows_all * fs, width), F32),
            pltpu.VMEM((rows_all * fs, width), F32),
            pltpu.VMEM((nb, rows, ch, width), F32),
            pltpu.VMEM((nb, rows, ch, width), F32),
            pltpu.VMEM((rows_all, ch, width), BF16),
            pltpu.VMEM((ch, bp), F32),
            pltpu.VMEM((64, ew), F32),
            pltpu.VMEM((nd, 8, ew // lane_parts), F32),
            pltpu.VMEM((nd, nb, 8, ew // lane_parts), F32),
            pltpu.VMEM((64, ew), F32),
            pltpu.VMEM((nb, 64, ew), F32),
            pltpu.VMEM((64, lw), F32),
            pltpu.VMEM((nd, 8, lw // lane_parts), F32),
            pltpu.VMEM((nd, 8, lw // lane_parts), F32),
            sems(nb, chunks), sems(nb, chunks), sems(nb, chunks), sems(nb, chunks),
            sems(nb), sems(nb), *[pltpu.SemaphoreType.DMA] * 8,
        ],
        compiler_params=pltpu.CompilerParams(
            collective_id=0, has_side_effects=True, vmem_limit_bytes=56 * 1024 * 1024
        ),
    )(
        image, kernel_taps.transpose(1, 2, 0), w_first.T, w_mid, w_out,
        target[0].reshape(outs * rows, width), mask[0],
    )
    g_taps, g_first, g_mid, g_out = pl.pallas_call(
        finish,
        out_shape=(
            jax.ShapeDtypeStruct((ks, ks, bands), F32),
            jax.ShapeDtypeStruct((ch, bands * nb), F32),
            jax.ShapeDtypeStruct((ch, ch), F32),
            jax.ShapeDtypeStruct((ch, outs), F32),
        ),
        in_specs=[vmem] * 4,
        out_specs=(vmem,) * 4,
    )(*sums)
    return (g_taps.transpose(2, 0, 1), g_first.T, g_mid, g_out)


def solution(mesh):
    in_specs = (
        P("dp", "band", None, None),
        P("band", None, None),
        P(),
        P(),
        P(),
        P("dp", None, "band", None),
        P("dp", "band", None),
    )
    out_specs = (P("band", None, None), P(), P(), P())
    return jax.shard_map(
        functools.partial(on_device, mesh.shape["dp"], mesh.shape["band"]),
        mesh=mesh, in_specs=in_specs, out_specs=out_specs, check_vma=False,
    )
```

```python
import functools
import math

import jax
import jax.numpy as jnp
from jax import lax
from jax.experimental import pallas as pl
from jax.experimental.pallas import tpu as pltpu
from jax.sharding import PartitionSpec as P

MESH = pl.DeviceIdType.MESH
F32 = jnp.float32
BF16 = jnp.bfloat16


def up(value, step):
    return -(-value // step) * step


def mm(a, b):
    return jnp.dot(a, b, preferred_element_type=F32)


def mm_tn(a, b):
    return lax.dot_general(a, b, (((0,), (0,)), ((), ())), preferred_element_type=F32)


def eye(n):
    same = lax.broadcasted_iota(jnp.int32, (n, n), 0) == lax.broadcasted_iota(jnp.int32, (n, n), 1)
    return jnp.where(same, 1.0, 0.0).astype(BF16)


def mm_nt(a, b):
    return lax.dot_general(a, b, (((1,), (1,)), ((), ())), preferred_element_type=F32)


def kernel(
    cfg,
    x_ref, taps_ref, w1t_ref, wm_ref, wo_ref, target_ref, mask_ref,
    gk_ref, gf_ref, gm_ref, go_ref,
    band_mask, edge, diag_mask, tap_rows, taps_own, wft_ref, wf_ref, wmt_ref, wot_ref, wanted, sums, stack, filt, slope, z_send, z_recv, dz_all, hid_s,
    early, early_in, early_out, total_ref, sides, late, late_in, late_out,
    z_ss, z_rs, d_ss, d_rs, ex_ss, ex_rs, e_ss, e_rs, ea_ss, ea_rs, l_ss, l_rs, la_ss, la_rs,
):
    nd, nb = cfg["nd"], cfg["nb"]
    bands, unroll, bp, ks = cfg["bands"], cfg["unroll"], cfg["bp"], cfg["ks"]
    fs, ts = cfg["fs"], cfg["ts"]
    rows_all, rows, width, chunks = cfg["rows_all"], cfg["rows"], cfg["width"], cfg["chunks"]
    ch, outs, scale = cfg["ch"], cfg["outs"], cfg["scale"]
    ew, lw = cfg["ew"], cfg["lw"]
    half = ks // 2
    lanes = 8 * rows_all
    step_rows = rows // chunks
    me_d = lax.axis_index("dp")
    me_b = lax.axis_index("band")
    split = nb == 2

    def each(count, act):
        if count <= 16:
            for k in range(1, count):
                act(k)
            return

        def body(k, _):
            act(k)
            return 0

        lax.fori_loop(1, count, body, 0)

    def crop_peer(k):
        return (lax.rem(me_d + k, nd), me_b)

    def band_peer(k):
        return (me_d, lax.rem(me_b + k, nb))

    barrier = pltpu.get_barrier_semaphore()

    def greet(peer):
        pl.semaphore_signal(barrier, inc=1, device_id=peer, device_id_type=MESH)

    each(nd, lambda k: greet(crop_peer(k)))
    each(nb, lambda k: greet(band_peer(k)))

    row_i = lax.broadcasted_iota(jnp.int32, (rows_all, lanes), 0)
    lane_i = lax.broadcasted_iota(jnp.int32, (rows_all, lanes), 1)
    block = lane_i // rows_all
    tap = lane_i % rows_all - row_i + half
    band_mask[...] = jnp.where((tap >= 0) & (tap < ks) & (block < ks), 1.0, 0.0)
    col = lax.broadcasted_iota(jnp.int32, (rows_all, width), 1)
    for j in range(ks):
        inside = (col + (j - half) >= 0) & (col + (j - half) < width)
        edge[j] = jnp.where(inside, 1.0, 0.0).astype(BF16)
    for h in range(rows_all):
        filt[pl.ds(h * fs + bp - 16, 16), :] = jnp.zeros((16, width), F32)

    place_j = lax.broadcasted_iota(jnp.int32, (ks, lanes), 0)
    place_l = lax.broadcasted_iota(jnp.int32, (ks, lanes), 1) - (8 - half)
    base = jnp.zeros((bands, lanes), F32)
    for i in range(ks):
        spot = jnp.where(place_l == place_j * rows_all + i, 1.0, 0.0).astype(BF16)
        base = base + mm_tn(taps_ref[i], spot)
    tap_rows[0:bands, :] = base

    lower = me_b == 0
    mid_row = rows_all // 2

    def filter_band(b):
        image = x_ref[b]
        parts = []
        for j in range(ks):
            s = j - half
            if s == 0:
                moved = image
            else:
                moved = pltpu.roll(image, (-s) % width, 1) * edge[j]
            parts.append(moved)
        parts.append(jnp.zeros((lanes - ks * rows_all, width), BF16))
        moved_all = jnp.concatenate(parts, axis=0)
        stack[b] = moved_all
        spread = jnp.broadcast_to(tap_rows[pl.ds(b, 1), :], (rows_all, lanes))
        taps = pltpu.roll(spread, lanes - 8, 1, stride=1, stride_axis=0)
        taps = taps * band_mask[...]
        if split:
            taps_own[b] = jnp.where(lower, taps[:mid_row], taps[mid_row:]).astype(BF16)
            taps = jnp.where(lower, taps[mid_row:], taps[:mid_row])
            first, count = (1 - me_b) * rows, rows
        else:
            first, count = 0, rows_all
        out = mm(taps.astype(BF16), moved_all)
        filt[pl.ds(first * fs + b, count, stride=fs), :] = out.astype(BF16).astype(F32)

    def filter_own(b):
        out = mm(taps_own[b], stack[b])
        filt[pl.ds(me_b * rows * fs + b, rows, stride=fs), :] = out.astype(BF16).astype(F32)

    def over_bands(lo, hi, act):
        def body(g, _):
            for q in range(unroll):
                act(g * unroll + q)
            return 0

        lax.fori_loop(lo, hi, body, 0)

    groups = bands // unroll
    over_bands(0, groups, filter_band)

    pick = jnp.where(
        lax.broadcasted_iota(jnp.int32, (bp, outs), 1)
        == lax.broadcasted_iota(jnp.int32, (bp, outs), 0) + me_b * bands,
        1.0, 0.0,
    )
    pick = jnp.where(lax.broadcasted_iota(jnp.int32, (bp, outs), 0) < bands, pick, 0.0).astype(BF16)
    wft_ref[...] = mm_nt(w1t_ref[...], pick).astype(BF16)

    def filt_rows(h, count):
        return jnp.concatenate(
            [
                filt[pl.ds(pl.multiple_of((h + r) * fs, 8), bp), :].astype(BF16)
                for r in range(count)
            ],
            axis=1,
        )

    pl.semaphore_wait(barrier, nd + nb - 2)

    def z_copy(k, c):
        part = pl.ds(c * step_rows, step_rows)
        return pltpu.make_async_remote_copy(
            src_ref=z_send.at[k, part],
            dst_ref=z_recv.at[k, part],
            send_sem=z_ss.at[k, c],
            recv_sem=z_rs.at[k, c],
            device_id=(me_d, lax.rem(me_b + k, nb)),
            device_id_type=MESH,
        )

    def z_part(k, c):
        owner = lax.rem(me_b + k, nb)

        h = c * step_rows
        z = mm(wft_ref[...], filt_rows(owner * rows + h, step_rows))
        for r in range(step_rows):
            z_send[k, h + r] = z[:, r * width:(r + 1) * width]

    for k in range(1, nb):
        for c in range(chunks):
            z_part(k, c)
            z_copy(k, c).start()
    if split:
        over_bands(0, groups, filter_own)
    for c in range(chunks):
        z_part(0, c)
    wf_ref[...] = mm_nt(pick, w1t_ref[...]).astype(BF16)
    wmt_ref[...] = mm_nt(eye(ch), wm_ref[...]).astype(BF16)
    wot_ref[...] = mm_nt(eye(outs), wo_ref[...]).astype(BF16)
    if ts == rows:
        wanted[...] = target_ref[...].astype(F32)
    else:
        def widen(g, _):
            for q in range(8):
                o = g * 8 + q
                block_o = target_ref[pl.ds(pl.multiple_of(o * rows, 16), rows), :]
                wanted[pl.ds(pl.multiple_of(o * ts, 8), rows), :] = block_o.astype(F32)
            return 0

        lax.fori_loop(0, outs // 8, widen, 0)

    def d_copy(k, c):
        part = pl.ds(me_b * rows + c * step_rows, step_rows)
        return pltpu.make_async_remote_copy(
            src_ref=dz_all.at[part],
            dst_ref=dz_all.at[part],
            send_sem=d_ss.at[k, c],
            recv_sem=d_rs.at[k, c],
            device_id=(me_d, lax.rem(me_b + k, nb)),
            device_id_type=MESH,
        )

    def wide(pieces):
        return jnp.concatenate(pieces, axis=1)

    g_out = jnp.zeros((ch, outs), F32)
    g_mid = jnp.zeros((ch, ch), F32)
    for c in range(chunks):
        for k in range(1, nb):
            z_copy(k, c).wait_recv()
        z_list = []
        for r in range(step_rows):
            h = c * step_rows + r
            z = z_send[0, h]
            for k in range(1, nb):
                z = z + z_recv[k, h]
            z_list.append(z)
        z_first = wide(z_list)
        sig_first = jax.nn.sigmoid(z_first)
        hid_first = (z_first * sig_first).astype(BF16)
        z_mid = mm(wmt_ref[...], hid_first)
        sig_mid = jax.nn.sigmoid(z_mid)
        hid_mid = (hid_first.astype(F32) + z_mid * sig_mid).astype(BF16)
        predicted = mm(wot_ref[...], hid_mid)
        errs = []
        for r in range(step_rows):
            h = c * step_rows + r
            factor = (2.0 * scale) * mask_ref[pl.ds(h, 1), :].astype(F32)
            diff = predicted[:, r * width:(r + 1) * width] - wanted[pl.ds(h, outs, stride=ts), :]
            errs.append((factor * diff).astype(BF16))
        err = wide(errs)
        g_out = g_out + mm_nt(hid_mid, err)
        d_mid = mm(wo_ref[...], err)
        dz_mid = (d_mid * (sig_mid * (1.0 + z_mid * (1.0 - sig_mid)))).astype(BF16)
        g_mid = g_mid + mm_nt(hid_first, dz_mid)
        d_first = d_mid + mm(wm_ref[...], dz_mid)
        dz = (d_first * (sig_first * (1.0 + z_first * (1.0 - sig_first)))).astype(BF16)
        for r in range(step_rows):
            h = c * step_rows + r
            dz_all[me_b * rows + h] = dz[:, r * width:(r + 1) * width]
        for k in range(1, nb):
            d_copy(k, c).start()

    def piece(ref, index, w):
        lane_parts = nd // 8
        each_w = w // lane_parts
        return ref.at[
            pl.ds(pl.multiple_of((index // lane_parts) * 8, 8), 8),
            pl.ds(pl.multiple_of(lax.rem(index, lane_parts) * each_w, 128), each_w),
        ]

    def remote(src, dst, ss, rs, peer):
        return pltpu.make_async_remote_copy(
            src_ref=src, dst_ref=dst, send_sem=ss, recv_sem=rs,
            device_id=peer, device_id_type=MESH,
        )

    def scatter(ref, into, w, ss, rs):
        def start(k):
            peer = crop_peer(k)
            remote(piece(ref, peer[0], w), into.at[k], ss, rs, peer).start()

        each(nd, start)

    def gather(out, ss, rs):
        def start(k):
            remote(out.at[me_d], out.at[me_d], ss, rs, crop_peer(k)).start()

        each(nd, start)

    def wait_all(ref, sem):
        rest = ref.at[pl.ds(1, nd - 1)]
        pltpu.make_async_copy(rest, rest, sem).wait()

    def add_up(ref, into, w):
        own = piece(ref, me_d, w)[...]
        for k in range(1, nd):
            own = own + into[k]
        return own

    def band_early(k):
        return remote(
            early_out.at[me_d, me_b], early_out.at[me_d, me_b], ex_ss.at[k], ex_rs.at[k], band_peer(k)
        )

    def spread_out(out, w, put):
        lane_parts = nd // 8
        each_w = w // lane_parts
        for d in range(nd):
            put(out, d, (d // lane_parts) * 8, (d % lane_parts) * each_w, each_w)

    early[...] = jnp.zeros_like(early)
    late[...] = jnp.zeros_like(late)
    sums[...] = jnp.zeros_like(sums)

    hid_s[...] = jnp.zeros_like(hid_s)

    def slope_rows(first):
        dz = wide([dz_all[first + r] for r in range(step_rows)])
        hid_s[...] += mm_nt(dz, filt_rows(first, step_rows))
        back = mm(wf_ref[...], dz)
        for r in range(step_rows):
            place = pl.multiple_of((rows_all - 1 - first - r) * fs, 8)
            slope[pl.ds(place, bp), :] = back[:, r * width:(r + 1) * width]

    skew = lanes - (rows_all - 1) + half
    extra = -skew % 8

    lane = lax.rem(lane_i + (lanes - extra), lanes)
    tap_e = lane % rows_all
    source_e = rows_all - 1 - row_i + tap_e - half
    valid = (lane < ks * rows_all) & (tap_e < ks) & (source_e >= 0) & (source_e < rows_all)
    diag_mask[...] = jnp.where(valid, 1.0, 0.0)

    def taps_band(b):
        rows_b = slope[pl.ds(b, rows_all, stride=fs), :].astype(BF16)
        cross = mm_nt(rows_b, stack[b])
        moved = pltpu.roll(cross, (skew + extra) % lanes, 1, stride=1, stride_axis=0)
        moved = moved * diag_mask[...]
        acc = moved[0:8]
        for r in range(8, rows_all, 8):
            acc = acc + moved[r:r + 8]
        for part in range(lanes // 128):
            sums[part, pl.ds(pl.multiple_of(b * 8, 8), 8), :] = acc[:, part * 128:(part + 1) * 128]

    for c in range(chunks):
        slope_rows(me_b * rows + c * step_rows)
    for k in range(1, nb):
        source = lax.rem(me_b + nb - k, nb)
        for c in range(chunks):
            d_copy(k, c).wait_recv()
            slope_rows(source * rows + c * step_rows)

    early[:, 0:outs] = g_out
    early[:, outs:outs + ch] = g_mid
    early[:, outs + ch:outs + ch + bands] = hid_s[:, 0:bands]
    scatter(early, early_in, ew, e_ss, e_rs)

    first, second = groups * 2 // 5, groups * 7 // 10
    over_bands(0, first, taps_band)

    wait_all(early_in, e_rs)
    early_out[me_d, me_b] = add_up(early, early_in, ew)
    for k in range(1, nb):
        band_early(k).start()

    over_bands(first, second, taps_band)

    for k in range(1, nb):
        band_early(k).wait_recv()
    gather(early_out, ea_ss, ea_rs)

    over_bands(second, groups, taps_band)

    slot_r = lax.broadcasted_iota(jnp.int32, (8 * ks, lanes), 0)
    slot_l = lax.broadcasted_iota(jnp.int32, (8 * ks, lanes), 1) - extra
    spot = jnp.where(slot_l == (slot_r % 8) * rows_all + slot_r // 8, 1.0, 0.0)
    parts = []
    for part in range(lanes // 128):
        rows_sum = sums[part, pl.ds(0, bp, stride=8), :]
        for r in range(1, 8):
            rows_sum = rows_sum + sums[part, pl.ds(r, bp, stride=8), :]
        parts.append(rows_sum)
    per_band = wide(parts)
    late[0:8 * ks, 0:bp] = lax.dot_general(
        spot, per_band, (((1,), (1,)), ((), ())),
        preferred_element_type=F32, precision=lax.Precision.HIGHEST,
    )
    scatter(late, late_in, lw, l_ss, l_rs)

    wait_all(early_out, ea_rs)

    def put_early(out, d, r, w0, w):
        both = out[d, 0]
        for k in range(1, nb):
            both = both + out[d, k]
        total_ref[r:r + 8, w0:w0 + w] = both
        for k in range(nb):
            sides[k, r:r + 8, w0:w0 + w] = out[d, k]

    spread_out(early_out, ew, put_early)
    go_ref[...] = total_ref[:, 0:outs]
    gm_ref[...] = total_ref[:, outs:outs + ch]
    for k in range(nb):
        gf_ref[:, k * bands:(k + 1) * bands] = sides[k, :, outs + ch:outs + ch + bands]

    wait_all(late_in, l_rs)
    late_out[me_d] = add_up(late, late_in, lw)
    gather(late_out, la_ss, la_rs)
    for k in range(1, nb):
        band_early(k).wait_send()
        for c in range(chunks):
            z_copy(k, c).wait_send()
            d_copy(k, c).wait_send()
    wait_all(early_in, e_ss)
    wait_all(early_out, ea_ss)
    wait_all(late_in, l_ss)
    wait_all(late_out, la_rs)

    def put_late(out, d, r, w0, w):
        gk_ref[r:r + 8, w0:w0 + w] = out[d]

    spread_out(late_out, lw, put_late)
    wait_all(late_out, la_ss)


def finish(gk_in, gf_in, gm_in, go_in, gk_out, gf_out, gm_out, go_out):
    ks, _, bands = gk_out.shape
    for i in range(ks):
        gk_out[i] = gk_in[8 * i:8 * i + ks, 0:bands]
    gf_out[...] = gf_in[...]
    gm_out[...] = gm_in[...]
    go_out[...] = go_in[...]


def on_device(nd, nb, radiance, kernel_taps, w_first, w_mid, w_out, target, mask):
    image = radiance[0]
    bands, rows_all, width = image.shape
    ks = kernel_taps.shape[1]
    ch = w_first.shape[1]
    outs = w_out.shape[1]
    rows = rows_all // nb
    chunks = min(2, rows // 2)
    unroll = max(u for u in range(1, 11) if bands % u == 0)
    bp = up(bands, 16)
    fs = bp + 8
    ts = rows + 8 if rows % 16 == 0 and outs % 8 == 0 else rows
    lane_parts = nd // 8
    lanes = 8 * rows_all
    ew = up(outs + ch + bands, 128 * lane_parts)
    lw = up(bp, 128 * lane_parts)
    cfg = dict(
        nd=nd, nb=nb, bands=bands, unroll=unroll, bp=bp, ks=ks, rows_all=rows_all, rows=rows,
        width=width, chunks=chunks, ch=ch, outs=outs, ew=ew, lw=lw, fs=fs, ts=ts,
        scale=1.0 / math.sqrt(nd * rows_all * width),
    )
    sems = lambda *shape: pltpu.SemaphoreType.DMA(shape)
    vmem = pl.BlockSpec(memory_space=pltpu.VMEM)
    sums = pl.pallas_call(
        functools.partial(kernel, cfg),
        out_shape=(
            jax.ShapeDtypeStruct((64, lw), F32),
            jax.ShapeDtypeStruct((ch, bands * nb), F32),
            jax.ShapeDtypeStruct((ch, ch), F32),
            jax.ShapeDtypeStruct((ch, outs), F32),
        ),
        in_specs=[vmem] * 7,
        out_specs=(vmem,) * 4,
        scratch_shapes=[
            pltpu.VMEM((rows_all, lanes), F32),
            pltpu.VMEM((ks, rows_all, width), BF16),
            pltpu.VMEM((rows_all, lanes), F32),
            pltpu.VMEM((bp, lanes), F32),
            pltpu.VMEM((bands, rows_all // 2, lanes), BF16),
            pltpu.VMEM((ch, bp), BF16),
            pltpu.VMEM((bp, ch), BF16),
            pltpu.VMEM((ch, ch), BF16),
            pltpu.VMEM((outs, ch), BF16),
            pltpu.VMEM((outs * ts, width), F32),
            pltpu.VMEM((lanes // 128, 8 * bp, 128), F32),
            pltpu.VMEM((bands, lanes, width), BF16),
            pltpu.VMEM((rows_all * fs, width), F32),
            pltpu.VMEM((rows_all * fs, width), F32),
            pltpu.VMEM((nb, rows, ch, width), F32),
            pltpu.VMEM((nb, rows, ch, width), F32),
            pltpu.VMEM((rows_all, ch, width), BF16),
            pltpu.VMEM((ch, bp), F32),
            pltpu.VMEM((64, ew), F32),
            pltpu.VMEM((nd, 8, ew // lane_parts), F32),
            pltpu.VMEM((nd, nb, 8, ew // lane_parts), F32),
            pltpu.VMEM((64, ew), F32),
            pltpu.VMEM((nb, 64, ew), F32),
            pltpu.VMEM((64, lw), F32),
            pltpu.VMEM((nd, 8, lw // lane_parts), F32),
            pltpu.VMEM((nd, 8, lw // lane_parts), F32),
            sems(nb, chunks), sems(nb, chunks), sems(nb, chunks), sems(nb, chunks),
            sems(nb), sems(nb), *[pltpu.SemaphoreType.DMA] * 8,
        ],
        compiler_params=pltpu.CompilerParams(
            collective_id=0, has_side_effects=True, vmem_limit_bytes=56 * 1024 * 1024
        ),
    )(
        image, kernel_taps.transpose(1, 2, 0), w_first.T, w_mid, w_out,
        target[0].reshape(outs * rows, width), mask[0],
    )
    g_taps, g_first, g_mid, g_out = pl.pallas_call(
        finish,
        out_shape=(
            jax.ShapeDtypeStruct((ks, ks, bands), F32),
            jax.ShapeDtypeStruct((ch, bands * nb), F32),
            jax.ShapeDtypeStruct((ch, ch), F32),
            jax.ShapeDtypeStruct((ch, outs), F32),
        ),
        in_specs=[vmem] * 4,
        out_specs=(vmem,) * 4,
    )(*sums)
    return (g_taps.transpose(2, 0, 1), g_first.T, g_mid, g_out)


def solution(mesh):
    in_specs = (
        P("dp", "band", None, None),
        P("band", None, None),
        P(),
        P(),
        P(),
        P("dp", None, "band", None),
        P("dp", "band", None),
    )
    out_specs = (P("band", None, None), P(), P(), P())
    return jax.shard_map(
        functools.partial(on_device, mesh.shape["dp"], mesh.shape["band"]),
        mesh=mesh, in_specs=in_specs, out_specs=out_specs, check_vma=False,
    )
```

```python
import functools
import math

import jax
import jax.numpy as jnp
from jax import lax
from jax.experimental import pallas as pl
from jax.experimental.pallas import tpu as pltpu
from jax.sharding import PartitionSpec as P

MESH = pl.DeviceIdType.MESH
F32 = jnp.float32
BF16 = jnp.bfloat16


def up(value, step):
    return -(-value // step) * step


def mm(a, b):
    return jnp.dot(a, b, preferred_element_type=F32)


def mm_tn(a, b):
    return lax.dot_general(a, b, (((0,), (0,)), ((), ())), preferred_element_type=F32)


def eye(n):
    same = lax.broadcasted_iota(jnp.int32, (n, n), 0) == lax.broadcasted_iota(jnp.int32, (n, n), 1)
    return jnp.where(same, 1.0, 0.0).astype(BF16)


def mm_nt(a, b):
    return lax.dot_general(a, b, (((1,), (1,)), ((), ())), preferred_element_type=F32)


def kernel(
    cfg,
    x_ref, taps_ref, w1t_ref, wm_ref, wo_ref, target_ref, mask_ref,
    gk_ref, gf_ref, gm_ref, go_ref,
    band_mask, edge, diag_mask, tap_rows, taps_own, wft_ref, wf_ref, wmt_ref, wot_ref, wanted, sums, stack, filt, slope, z_send, z_recv, dz_all, hid_s,
    early, early_in, early_out, total_ref, sides, late, late_in, late_out,
    z_ss, z_rs, d_ss, d_rs, ex_ss, ex_rs, e_ss, e_rs, ea_ss, ea_rs, l_ss, l_rs, la_ss, la_rs,
):
    nd, nb = cfg["nd"], cfg["nb"]
    bands, unroll, bp, ks = cfg["bands"], cfg["unroll"], cfg["bp"], cfg["ks"]
    fs, ts = cfg["fs"], cfg["ts"]
    rows_all, rows, width, chunks = cfg["rows_all"], cfg["rows"], cfg["width"], cfg["chunks"]
    ch, outs, scale = cfg["ch"], cfg["outs"], cfg["scale"]
    ew, lw = cfg["ew"], cfg["lw"]
    half = ks // 2
    lanes = 8 * rows_all
    step_rows = rows // chunks
    me_d = lax.axis_index("dp")
    me_b = lax.axis_index("band")
    split = nb == 2

    def each(count, act):
        if count <= 16:
            for k in range(1, count):
                act(k)
            return

        def body(k, _):
            act(k)
            return 0

        lax.fori_loop(1, count, body, 0)

    def crop_peer(k):
        return (lax.rem(me_d + k, nd), me_b)

    def band_peer(k):
        return (me_d, lax.rem(me_b + k, nb))

    barrier = pltpu.get_barrier_semaphore()

    def greet(peer):
        pl.semaphore_signal(barrier, inc=1, device_id=peer, device_id_type=MESH)

    each(nd, lambda k: greet(crop_peer(k)))
    each(nb, lambda k: greet(band_peer(k)))

    row_i = lax.broadcasted_iota(jnp.int32, (rows_all, lanes), 0)
    lane_i = lax.broadcasted_iota(jnp.int32, (rows_all, lanes), 1)
    block = lane_i // rows_all
    tap = lane_i % rows_all - row_i + half
    band_mask[...] = jnp.where((tap >= 0) & (tap < ks) & (block < ks), 1.0, 0.0)
    col = lax.broadcasted_iota(jnp.int32, (rows_all, width), 1)
    for j in range(ks):
        inside = (col + (j - half) >= 0) & (col + (j - half) < width)
        edge[j] = jnp.where(inside, 1.0, 0.0).astype(BF16)
    for h in range(rows_all):
        filt[pl.ds(h * fs + bp - 16, 16), :] = jnp.zeros((16, width), F32)

    place_j = lax.broadcasted_iota(jnp.int32, (ks, lanes), 0)
    place_l = lax.broadcasted_iota(jnp.int32, (ks, lanes), 1) - (8 - half)
    base = jnp.zeros((bands, lanes), F32)
    for i in range(ks):
        spot = jnp.where(place_l == place_j * rows_all + i, 1.0, 0.0).astype(BF16)
        base = base + mm_tn(taps_ref[i], spot)
    tap_rows[0:bands, :] = base

    lower = me_b == 0
    mid_row = rows_all // 2

    def filter_band(b):
        image = x_ref[b]
        parts = []
        for j in range(ks):
            s = j - half
            if s == 0:
                moved = image
            else:
                moved = pltpu.roll(image, (-s) % width, 1) * edge[j]
            parts.append(moved)
        parts.append(jnp.zeros((lanes - ks * rows_all, width), BF16))
        moved_all = jnp.concatenate(parts, axis=0)
        stack[b] = moved_all
        spread = jnp.broadcast_to(tap_rows[pl.ds(b, 1), :], (rows_all, lanes))
        taps = pltpu.roll(spread, lanes - 8, 1, stride=1, stride_axis=0)
        taps = taps * band_mask[...]
        if split:
            taps_own[b] = jnp.where(lower, taps[:mid_row], taps[mid_row:]).astype(BF16)
            taps = jnp.where(lower, taps[mid_row:], taps[:mid_row])
            first, count = (1 - me_b) * rows, rows
        else:
            first, count = 0, rows_all
        out = mm(taps.astype(BF16), moved_all)
        filt[pl.ds(first * fs + b, count, stride=fs), :] = out.astype(BF16).astype(F32)

    def filter_own(b):
        out = mm(taps_own[b], stack[b])
        filt[pl.ds(me_b * rows * fs + b, rows, stride=fs), :] = out.astype(BF16).astype(F32)

    def over_bands(lo, hi, act):
        def body(g, _):
            for q in range(unroll):
                act(g * unroll + q)
            return 0

        lax.fori_loop(lo, hi, body, 0)

    groups = bands // unroll
    over_bands(0, groups, filter_band)

    pick = jnp.where(
        lax.broadcasted_iota(jnp.int32, (bp, outs), 1)
        == lax.broadcasted_iota(jnp.int32, (bp, outs), 0) + me_b * bands,
        1.0, 0.0,
    )
    pick = jnp.where(lax.broadcasted_iota(jnp.int32, (bp, outs), 0) < bands, pick, 0.0).astype(BF16)
    wft_ref[...] = mm_nt(w1t_ref[...], pick).astype(BF16)

    def filt_rows(h, count):
        return jnp.concatenate(
            [
                filt[pl.ds(pl.multiple_of((h + r) * fs, 8), bp), :].astype(BF16)
                for r in range(count)
            ],
            axis=1,
        )

    pl.semaphore_wait(barrier, nd + nb - 2)

    def z_copy(k, c):
        part = pl.ds(c * step_rows, step_rows)
        return pltpu.make_async_remote_copy(
            src_ref=z_send.at[k, part],
            dst_ref=z_recv.at[k, part],
            send_sem=z_ss.at[k, c],
            recv_sem=z_rs.at[k, c],
            device_id=(me_d, lax.rem(me_b + k, nb)),
            device_id_type=MESH,
        )

    def z_part(k, c):
        owner = lax.rem(me_b + k, nb)

        h = c * step_rows
        z = mm(wft_ref[...], filt_rows(owner * rows + h, step_rows))
        for r in range(step_rows):
            z_send[k, h + r] = z[:, r * width:(r + 1) * width]

    for k in range(1, nb):
        for c in range(chunks):
            z_part(k, c)
            z_copy(k, c).start()
    if split:
        over_bands(0, groups, filter_own)
    for c in range(chunks):
        z_part(0, c)
    wf_ref[...] = mm_nt(pick, w1t_ref[...]).astype(BF16)
    wmt_ref[...] = mm_nt(eye(ch), wm_ref[...]).astype(BF16)
    wot_ref[...] = mm_nt(eye(outs), wo_ref[...]).astype(BF16)
    if ts == rows:
        wanted[...] = target_ref[...].astype(F32)
    else:
        def widen(g, _):
            for q in range(8):
                o = g * 8 + q
                block_o = target_ref[pl.ds(pl.multiple_of(o * rows, 16), rows), :]
                wanted[pl.ds(pl.multiple_of(o * ts, 8), rows), :] = block_o.astype(F32)
            return 0

        lax.fori_loop(0, outs // 8, widen, 0)

    def d_copy(k, c):
        part = pl.ds(me_b * rows + c * step_rows, step_rows)
        return pltpu.make_async_remote_copy(
            src_ref=dz_all.at[part],
            dst_ref=dz_all.at[part],
            send_sem=d_ss.at[k, c],
            recv_sem=d_rs.at[k, c],
            device_id=(me_d, lax.rem(me_b + k, nb)),
            device_id_type=MESH,
        )

    def wide(pieces):
        return jnp.concatenate(pieces, axis=1)

    g_out = jnp.zeros((ch, outs), F32)
    g_mid = jnp.zeros((ch, ch), F32)
    for c in range(chunks):
        for k in range(1, nb):
            z_copy(k, c).wait_recv()
        z_list = []
        for r in range(step_rows):
            h = c * step_rows + r
            z = z_send[0, h]
            for k in range(1, nb):
                z = z + z_recv[k, h]
            z_list.append(z)
        z_first = wide(z_list)
        sig_first = jax.nn.sigmoid(z_first)
        hid_first = (z_first * sig_first).astype(BF16)
        z_mid = mm(wmt_ref[...], hid_first)
        sig_mid = jax.nn.sigmoid(z_mid)
        hid_mid = (hid_first.astype(F32) + z_mid * sig_mid).astype(BF16)
        predicted = mm(wot_ref[...], hid_mid)
        errs = []
        for r in range(step_rows):
            h = c * step_rows + r
            factor = (2.0 * scale) * mask_ref[pl.ds(h, 1), :].astype(F32)
            diff = predicted[:, r * width:(r + 1) * width] - wanted[pl.ds(h, outs, stride=ts), :]
            errs.append((factor * diff).astype(BF16))
        err = wide(errs)
        g_out = g_out + mm_nt(hid_mid, err)
        d_mid = mm(wo_ref[...], err)
        dz_mid = (d_mid * (sig_mid * (1.0 + z_mid * (1.0 - sig_mid)))).astype(BF16)
        g_mid = g_mid + mm_nt(hid_first, dz_mid)
        d_first = d_mid + mm(wm_ref[...], dz_mid)
        dz = (d_first * (sig_first * (1.0 + z_first * (1.0 - sig_first)))).astype(BF16)
        for r in range(step_rows):
            h = c * step_rows + r
            dz_all[me_b * rows + h] = dz[:, r * width:(r + 1) * width]
        for k in range(1, nb):
            d_copy(k, c).start()

    def piece(ref, index, w):
        lane_parts = nd // 8
        each_w = w // lane_parts
        return ref.at[
            pl.ds(pl.multiple_of((index // lane_parts) * 8, 8), 8),
            pl.ds(pl.multiple_of(lax.rem(index, lane_parts) * each_w, 128), each_w),
        ]

    def remote(src, dst, ss, rs, peer):
        return pltpu.make_async_remote_copy(
            src_ref=src, dst_ref=dst, send_sem=ss, recv_sem=rs,
            device_id=peer, device_id_type=MESH,
        )

    def scatter(ref, into, w, ss, rs):
        def start(k):
            peer = crop_peer(k)
            remote(piece(ref, peer[0], w), into.at[k], ss, rs, peer).start()

        each(nd, start)

    def gather(out, ss, rs):
        def start(k):
            remote(out.at[me_d], out.at[me_d], ss, rs, crop_peer(k)).start()

        each(nd, start)

    def wait_all(ref, sem):
        rest = ref.at[pl.ds(1, nd - 1)]
        pltpu.make_async_copy(rest, rest, sem).wait()

    def add_up(ref, into, w):
        own = piece(ref, me_d, w)[...]
        for k in range(1, nd):
            own = own + into[k]
        return own

    def band_early(k):
        return remote(
            early_out.at[me_d, me_b], early_out.at[me_d, me_b], ex_ss.at[k], ex_rs.at[k], band_peer(k)
        )

    def spread_out(out, w, put):
        lane_parts = nd // 8
        each_w = w // lane_parts
        for d in range(nd):
            put(out, d, (d // lane_parts) * 8, (d % lane_parts) * each_w, each_w)

    early[...] = jnp.zeros_like(early)
    late[...] = jnp.zeros_like(late)
    sums[...] = jnp.zeros_like(sums)

    hid_s[...] = jnp.zeros_like(hid_s)

    def slope_rows(first):
        dz = wide([dz_all[first + r] for r in range(step_rows)])
        hid_s[...] += mm_nt(dz, filt_rows(first, step_rows))
        back = mm(wf_ref[...], dz)
        for r in range(step_rows):
            place = pl.multiple_of((rows_all - 1 - first - r) * fs, 8)
            slope[pl.ds(place, bp), :] = back[:, r * width:(r + 1) * width]

    skew = lanes - (rows_all - 1) + half
    extra = -skew % 8

    lane = lax.rem(lane_i + (lanes - extra), lanes)
    tap_e = lane % rows_all
    source_e = rows_all - 1 - row_i + tap_e - half
    valid = (lane < ks * rows_all) & (tap_e < ks) & (source_e >= 0) & (source_e < rows_all)
    diag_mask[...] = jnp.where(valid, 1.0, 0.0)

    def taps_band(b):
        rows_b = slope[pl.ds(b, rows_all, stride=fs), :].astype(BF16)
        cross = mm_nt(rows_b, stack[b])
        moved = pltpu.roll(cross, (skew + extra) % lanes, 1, stride=1, stride_axis=0)
        moved = moved * diag_mask[...]
        acc = moved[0:8]
        for r in range(8, rows_all, 8):
            acc = acc + moved[r:r + 8]
        for part in range(lanes // 128):
            sums[part, pl.ds(pl.multiple_of(b * 8, 8), 8), :] = acc[:, part * 128:(part + 1) * 128]

    for c in range(chunks):
        slope_rows(me_b * rows + c * step_rows)
    for k in range(1, nb):
        source = lax.rem(me_b + nb - k, nb)
        for c in range(chunks):
            d_copy(k, c).wait_recv()
            slope_rows(source * rows + c * step_rows)

    early[:, 0:outs] = g_out
    early[:, outs:outs + ch] = g_mid
    early[:, outs + ch:outs + ch + bands] = hid_s[:, 0:bands]
    scatter(early, early_in, ew, e_ss, e_rs)

    first, second = groups * 2 // 5, groups * 7 // 10
    over_bands(0, first, taps_band)

    wait_all(early_in, e_rs)
    early_out[me_d, me_b] = add_up(early, early_in, ew)
    for k in range(1, nb):
        band_early(k).start()

    over_bands(first, second, taps_band)

    for k in range(1, nb):
        band_early(k).wait_recv()
    gather(early_out, ea_ss, ea_rs)

    over_bands(second, groups, taps_band)

    slot_r = lax.broadcasted_iota(jnp.int32, (8 * ks, lanes), 0)
    slot_l = lax.broadcasted_iota(jnp.int32, (8 * ks, lanes), 1) - extra
    spot = jnp.where(slot_l == (slot_r % 8) * rows_all + slot_r // 8, 1.0, 0.0)
    parts = []
    for part in range(lanes // 128):
        rows_sum = sums[part, pl.ds(0, bp, stride=8), :]
        for r in range(1, 8):
            rows_sum = rows_sum + sums[part, pl.ds(r, bp, stride=8), :]
        parts.append(rows_sum)
    per_band = wide(parts)
    late[0:8 * ks, 0:bp] = lax.dot_general(
        spot, per_band, (((1,), (1,)), ((), ())),
        preferred_element_type=F32, precision=lax.Precision.HIGHEST,
    )
    scatter(late, late_in, lw, l_ss, l_rs)

    wait_all(early_out, ea_rs)

    def put_early(out, d, r, w0, w):
        both = out[d, 0]
        for k in range(1, nb):
            both = both + out[d, k]
        total_ref[r:r + 8, w0:w0 + w] = both
        for k in range(nb):
            sides[k, r:r + 8, w0:w0 + w] = out[d, k]

    spread_out(early_out, ew, put_early)
    go_ref[...] = total_ref[:, 0:outs]
    gm_ref[...] = total_ref[:, outs:outs + ch]
    for k in range(nb):
        gf_ref[:, k * bands:(k + 1) * bands] = sides[k, :, outs + ch:outs + ch + bands]

    wait_all(late_in, l_rs)
    late_out[me_d] = add_up(late, late_in, lw)
    gather(late_out, la_ss, la_rs)
    for k in range(1, nb):
        band_early(k).wait_send()
        for c in range(chunks):
            z_copy(k, c).wait_send()
            d_copy(k, c).wait_send()
    wait_all(early_in, e_ss)
    wait_all(early_out, ea_ss)
    wait_all(late_in, l_ss)
    wait_all(late_out, la_rs)

    def put_late(out, d, r, w0, w):
        gk_ref[r:r + 8, w0:w0 + w] = out[d]

    spread_out(late_out, lw, put_late)
    wait_all(late_out, la_ss)


def finish(gk_in, gf_in, gm_in, go_in, gk_out, gf_out, gm_out, go_out):
    ks, _, bands = gk_out.shape
    for i in range(ks):
        gk_out[i] = gk_in[8 * i:8 * i + ks, 0:bands]
    gf_out[...] = gf_in[...]
    gm_out[...] = gm_in[...]
    go_out[...] = go_in[...]


def on_device(nd, nb, radiance, kernel_taps, w_first, w_mid, w_out, target, mask):
    image = radiance[0]
    bands, rows_all, width = image.shape
    ks = kernel_taps.shape[1]
    ch = w_first.shape[1]
    outs = w_out.shape[1]
    rows = rows_all // nb
    chunks = min(4, rows // 2)
    unroll = max(u for u in range(1, 11) if bands % u == 0)
    bp = up(bands, 16)
    fs = bp + 8
    ts = rows + 8 if rows % 16 == 0 and outs % 8 == 0 else rows
    lane_parts = nd // 8
    lanes = 8 * rows_all
    ew = up(outs + ch + bands, 128 * lane_parts)
    lw = up(bp, 128 * lane_parts)
    cfg = dict(
        nd=nd, nb=nb, bands=bands, unroll=unroll, bp=bp, ks=ks, rows_all=rows_all, rows=rows,
        width=width, chunks=chunks, ch=ch, outs=outs, ew=ew, lw=lw, fs=fs, ts=ts,
        scale=1.0 / math.sqrt(nd * rows_all * width),
    )
    sems = lambda *shape: pltpu.SemaphoreType.DMA(shape)
    vmem = pl.BlockSpec(memory_space=pltpu.VMEM)
    sums = pl.pallas_call(
        functools.partial(kernel, cfg),
        out_shape=(
            jax.ShapeDtypeStruct((64, lw), F32),
            jax.ShapeDtypeStruct((ch, bands * nb), F32),
            jax.ShapeDtypeStruct((ch, ch), F32),
            jax.ShapeDtypeStruct((ch, outs), F32),
        ),
        in_specs=[vmem] * 7,
        out_specs=(vmem,) * 4,
        scratch_shapes=[
            pltpu.VMEM((rows_all, lanes), F32),
            pltpu.VMEM((ks, rows_all, width), BF16),
            pltpu.VMEM((rows_all, lanes), F32),
            pltpu.VMEM((bp, lanes), F32),
            pltpu.VMEM((bands, rows_all // 2, lanes), BF16),
            pltpu.VMEM((ch, bp), BF16),
            pltpu.VMEM((bp, ch), BF16),
            pltpu.VMEM((ch, ch), BF16),
            pltpu.VMEM((outs, ch), BF16),
            pltpu.VMEM((outs * ts, width), F32),
            pltpu.VMEM((lanes // 128, 8 * bp, 128), F32),
            pltpu.VMEM((bands, lanes, width), BF16),
            pltpu.VMEM((rows_all * fs, width), F32),
            pltpu.VMEM((rows_all * fs, width), F32),
            pltpu.VMEM((nb, rows, ch, width), F32),
            pltpu.VMEM((nb, rows, ch, width), F32),
            pltpu.VMEM((rows_all, ch, width), BF16),
            pltpu.VMEM((ch, bp), F32),
            pltpu.VMEM((64, ew), F32),
            pltpu.VMEM((nd, 8, ew // lane_parts), F32),
            pltpu.VMEM((nd, nb, 8, ew // lane_parts), F32),
            pltpu.VMEM((64, ew), F32),
            pltpu.VMEM((nb, 64, ew), F32),
            pltpu.VMEM((64, lw), F32),
            pltpu.VMEM((nd, 8, lw // lane_parts), F32),
            pltpu.VMEM((nd, 8, lw // lane_parts), F32),
            sems(nb, chunks), sems(nb, chunks), sems(nb, chunks), sems(nb, chunks),
            sems(nb), sems(nb), *[pltpu.SemaphoreType.DMA] * 8,
        ],
        compiler_params=pltpu.CompilerParams(
            collective_id=0, has_side_effects=True, vmem_limit_bytes=56 * 1024 * 1024
        ),
    )(
        image, kernel_taps.transpose(1, 2, 0), w_first.T, w_mid, w_out,
        target[0].reshape(outs * rows, width), mask[0],
    )
    g_taps, g_first, g_mid, g_out = pl.pallas_call(
        finish,
        out_shape=(
            jax.ShapeDtypeStruct((ks, ks, bands), F32),
            jax.ShapeDtypeStruct((ch, bands * nb), F32),
            jax.ShapeDtypeStruct((ch, ch), F32),
            jax.ShapeDtypeStruct((ch, outs), F32),
        ),
        in_specs=[vmem] * 4,
        out_specs=(vmem,) * 4,
    )(*sums)
    return (g_taps.transpose(2, 0, 1), g_first.T, g_mid, g_out)


def solution(mesh):
    in_specs = (
        P("dp", "band", None, None),
        P("band", None, None),
        P(),
        P(),
        P(),
        P("dp", None, "band", None),
        P("dp", "band", None),
    )
    out_specs = (P("band", None, None), P(), P(), P())
    return jax.shard_map(
        functools.partial(on_device, mesh.shape["dp"], mesh.shape["band"]),
        mesh=mesh, in_specs=in_specs, out_specs=out_specs, check_vma=False,
    )
```
